256 devices in a mesh: dp: 64 (over y, x, z_lo), tensor: 4 (over z_hi, core).
Axes of the slice: x: 4, y: 4, z: 8 (z_hi: 2, z_lo: 4; z = z_hi * 4 + z_lo), core: 2. Of those that a mesh axis runs over, the one named last changes fastest.
Arguments:
- attn_out: bfloat16 [8192, 4096], P('dp', 'tensor'), may hold values from -6 to 6
- out_proj: bfloat16 [4096, 4096], P('tensor', 'dp'), may hold values from -0.09375 to 0.09375
- residual: bfloat16 [8192, 4096], P('dp', 'tensor')
- teacher_gain: float32 [4096], P('tensor'), may hold values from 0.25 to 1.75
- student_feats: bfloat16 [57344, 1024], P('dp')
- head_small: bfloat16 [384, 4096], P(None, 'tensor'), may hold values from -0.3125 to 0.3125
- head_base: bfloat16 [768, 4096], P(None, 'tensor'), may hold values from -0.21875 to 0.21875
- head_large: bfloat16 [1024, 4096], P(None, 'tensor'), may hold values from -0.1875 to 0.1875
- gain_small: float32 [384], replicated, may hold values from 0.25 to 1.75
- gain_base: float32 [768], replicated, may hold values from 0.25 to 1.75
- gain_large: float32 [1024], replicated, may hold values from 0.25 to 1.75
- row_shard: int32 [8192, 3], P('dp'), may hold values from 0 to 63, as said below
Outputs:
- grad_head_small: float32 [384, 4096], P('dp', 'tensor')
- grad_head_base: float32 [768, 4096], P('dp', 'tensor')
- grad_head_large: float32 [1024, 4096], P('dp', 'tensor')
- grad_gain_small: float32 [384], P('tensor')
- grad_gain_base: float32 [768], P('tensor')
- grad_gain_large: float32 [1024], P('tensor')
- token_gradient: bfloat16 [57344, 1024], P('dp', 'tensor')
- losses: float32 [3], replicated
The draws below stay inside these ranges and needn't reach their ends.
Inputs may be any that keep to these rules, and one draw needn't show every extreme that they name: `row_shard`: column g names only shards of group g: 12, 20 and 32 distinct shards for g = 0, 1, 2, no shard in two columns, every shard in some column. In each column, of the 128 tokens of one index of dp at most 14 name one shard; in each column one shard is named by exactly min(14, 128 - G + 1) tokens of every index of dp (G the group's shard count), and every shard of the group by at least one token of every index of dp.
All inputs are finite; a program needn't handle non-finite values.
Results may differ from the reference program's by a relative error of at most 0.0072.
Values may be sent and summed in bfloat16 or wider, within the bound.
No kernel may reach another device: no remote copies, remote signals or barrier semaphores. Data moves between devices by JAX's collectives and lax.ppermute only.
A program may use at most 128 MiB of HBM per device.

```python
import math
import jax
import jax.numpy as jnp
from jax import lax

D = 4096
HQ = 4096
WS = 384
WB = 768
WL = 1024
ROWS_DEV = 128
TOKENS = 8192
GS = 12
GB = 20
GL = 32
SEND_CAP = 14
SLOTS = 896
STUDENT_ROWS = 57344
N_DP = 64
N_TENSOR = 4


def row_column_scales(key, rows, cols, lowest, highest):
    key_rows, key_cols = jax.random.split(key)
    row_scale = jnp.exp(jax.random.uniform(key_rows, (rows, 1), jnp.float32, math.log(lowest), math.log(highest)))
    col_scale = jnp.exp(jax.random.uniform(key_cols, (1, cols), jnp.float32, math.log(0.5), math.log(2.0)))
    rising = 0.6 + 1.2 * jnp.arange(cols, dtype=jnp.float32) / cols
    return row_scale * col_scale * rising


def uneven_field(key, rows, cols):
    key_base, key_scale = jax.random.split(key, 2)
    base = jax.random.normal(key_base, (rows, cols), jnp.float32)
    scales = row_column_scales(key_scale, rows, cols, 0.3, 3.0)
    return (base * scales).astype(jnp.bfloat16)


def draw_residual(key, part):
    key = jax.random.fold_in(key, 3)
    return uneven_field(key, TOKENS, D)


def draw_student_feats(key, part):
    key = jax.random.fold_in(key, 5)
    return uneven_field(key, STUDENT_ROWS, WL)


def shard_order(key):
    return jax.random.permutation(jax.random.fold_in(key, 101), N_DP).astype(jnp.int32)


def draw_row_shard(key, part):
    order = shard_order(key)
    key = jax.random.fold_in(key, 13)
    columns = []
    offset = 0
    for selected_index, group_size in enumerate((GS, GB, GL)):
        members = order[offset:offset + group_size]
        offset = offset + group_size
        busiest = members[0]
        if group_size > 1:
            others = members[1:]
        else:
            others = members
        spread = max(group_size - 1, 1)
        busy_quota = min(SEND_CAP, ROWS_DEV - group_size + 1)
        source_keys = jax.random.split(jax.random.fold_in(key, selected_index), N_DP)

        def one_source(source_key, others=others, busiest=busiest, spread=spread, busy_quota=busy_quota):
            key_rows, key_others = jax.random.split(source_key)
            position = jax.random.permutation(key_rows, ROWS_DEV).astype(jnp.int32)
            order_others = jax.random.permutation(key_others, spread).astype(jnp.int32)
            turn_index = jnp.maximum(position - busy_quota, 0) % spread
            others_pick = others[order_others[turn_index]]
            return jnp.where(position < busy_quota, busiest, others_pick)
        columns.append(jax.vmap(one_source)(source_keys).reshape(TOKENS))
    return jnp.stack(columns, axis=1).astype(jnp.int32)


def block_scale(own_key, extent, pieces, least, largest):
    gain, own = 1.0, jax.random.fold_in(own_key, 6)
    for axis_at, blocks in pieces:
        draws = jnp.exp(jax.random.uniform(jax.random.fold_in(own, axis_at), (blocks,), jnp.float32, least / len(pieces), largest / len(pieces)))
        gain = gain * jnp.repeat(draws, extent[axis_at] // blocks).reshape([-1 if axis == axis_at else 1 for axis in range(len(extent))])
    return gain


def bell_draw(key, extent, scale, reach, cuts=(), held_as=jnp.bfloat16):
    drawn = scale * jax.random.normal(key, extent, jnp.float32)
    if cuts:
        drawn = drawn * block_scale(key, extent, cuts, -0.22, 0.18)
    return jnp.clip(drawn, -reach, reach).astype(held_as)


def setup_inputs(seed: int = 0) -> dict:
    key_list = jax.random.split(jax.random.key(seed), 13)
    return {
        "attn_out": bell_draw(key_list[0], (TOKENS, HQ), 1.0, 6.0, ((0, 64), (1, 4))),
        "out_proj": bell_draw(key_list[1], (HQ, D), HQ ** -0.5, 0.09375, ((0, 4), (1, 64))),
        "residual": draw_residual(jax.random.fold_in(key_list[12], 71), 0),
        "teacher_gain": jnp.clip(1.0 + 0.15 * jax.random.normal(key_list[3], (D,), jnp.float32), 0.25, 1.75),
        "student_feats": draw_student_feats(jax.random.fold_in(key_list[12], 71), 0),
        "head_small": bell_draw(key_list[5], (WS, D), WS ** -0.5, 0.3125, ((1, 4),)),
        "head_base": bell_draw(key_list[6], (WB, D), WB ** -0.5, 0.21875, ((1, 4),)),
        "head_large": bell_draw(key_list[7], (WL, D), WL ** -0.5, 0.1875, ((1, 4),)),
        "gain_small": jnp.clip(1.0 + 0.15 * jax.random.normal(key_list[8], (WS,), jnp.float32), 0.25, 1.75),
        "gain_base": jnp.clip(1.0 + 0.15 * jax.random.normal(key_list[9], (WB,), jnp.float32), 0.25, 1.75),
        "gain_large": jnp.clip(1.0 + 0.15 * jax.random.normal(key_list[10], (WL,), jnp.float32), 0.25, 1.75),
        "row_shard": draw_row_shard(jax.random.fold_in(key_list[12], 71), 0),
    }


def row_norm_values(value_list):
    center = lax.optimization_barrier(jnp.mean(value_list, axis=1, keepdims=True))
    spread = lax.optimization_barrier(jnp.mean(value_list * value_list, axis=1, keepdims=True)) - center * center
    scale_factor = lax.rsqrt(spread + 1e-06)
    return ((value_list - center) * scale_factor, scale_factor)

def unblock(value_list, feature_width):
    blocks = value_list.reshape(value_list.shape[0], N_TENSOR, WL // N_TENSOR)
    return blocks[:, :, :feature_width // N_TENSOR].reshape(value_list.shape[0], feature_width)

def regroup_blocks(value_list):
    count, feature_width = value_list.shape
    blocks = value_list.reshape(count, N_TENSOR, feature_width // N_TENSOR)
    blocks = jnp.pad(blocks, ((0, 0), (0, 0), (0, WL // N_TENSOR - feature_width // N_TENSOR)))
    return blocks.reshape(count, WL)

def slot_index(column):
    blocks = column.reshape(N_DP, ROWS_DEV)
    shard_ids = jnp.arange(N_DP, dtype=jnp.int32)
    onehot = (blocks[:, :, None] == shard_ids[None, None, :]).astype(jnp.int32)
    earlier = jnp.cumsum(onehot, axis=1) - onehot
    rank = lax.optimization_barrier(jnp.sum(earlier * onehot, axis=2)).astype(jnp.int32)
    source = jnp.arange(N_DP, dtype=jnp.int32)[:, None]
    return (blocks * SLOTS + source * SEND_CAP + rank).reshape(TOKENS).astype(jnp.int32)

def student_pass(token_rows, gain_vector, head, target, weight):
    centered_scaled, scale_factor = row_norm_values(token_rows.astype(jnp.float32))
    normalized_rows = (centered_scaled * gain_vector).astype(jnp.bfloat16)
    student_out = jnp.dot(normalized_rows, head, preferred_element_type=jnp.float32)
    diff = student_out - target.astype(jnp.float32)
    error = (weight[:, None] * diff).astype(jnp.bfloat16)
    square_root = math.sqrt(TOKENS)
    grad_head = jnp.dot(normalized_rows.T, error, preferred_element_type=jnp.float32) / square_root
    backward_value = jnp.dot(error, head.T, preferred_element_type=jnp.float32)
    gain_gradient = lax.optimization_barrier(jnp.sum(backward_value * centered_scaled, axis=0)) / square_root
    feature_width = token_rows.shape[1]
    upper_limit = backward_value * gain_vector
    first_moment = lax.optimization_barrier(jnp.sum(upper_limit, axis=1, keepdims=True)) / feature_width
    second_moment = lax.optimization_barrier(jnp.sum(upper_limit * centered_scaled, axis=1, keepdims=True)) / feature_width
    row_gradient = (scale_factor * (upper_limit - first_moment - centered_scaled * second_moment)).astype(jnp.bfloat16)
    loss = jnp.sum(weight * lax.optimization_barrier(jnp.sum(diff * diff, axis=1))) / (2.0 * D * TOKENS)
    return (grad_head, gain_gradient, row_gradient, loss)

def reference(attn_out, out_proj, residual, teacher_gain, student_feats, head_small, head_base, head_large, gain_small, gain_base, gain_large, row_shard):
    hidden = residual.astype(jnp.float32) + jnp.dot(attn_out, out_proj, preferred_element_type=jnp.float32)
    center = lax.optimization_barrier(jnp.mean(hidden, axis=1, keepdims=True))
    spread = lax.optimization_barrier(jnp.mean(hidden * hidden, axis=1, keepdims=True)) - center * center
    target = ((hidden - center) * lax.rsqrt(spread + 1e-06) * teacher_gain).astype(jnp.bfloat16)
    group_sizes = (GS, GB, GL)
    widths = (WS, WB, WL)
    shard_ids = jnp.arange(N_DP, dtype=jnp.int32)
    heads = (head_small, head_base, head_large)
    gain_list = (gain_small, gain_base, gain_large)
    token_gradient = jnp.zeros((STUDENT_ROWS, WL), jnp.bfloat16)
    head_grads = []
    gain_grads = []
    loss_list = []
    for selected_index in range(3):
        column = row_shard[:, selected_index]
        onehot = (column[:, None] == shard_ids[None, :]).astype(jnp.float32)
        counts = lax.optimization_barrier(jnp.sum(onehot, axis=0))
        owned = lax.optimization_barrier(jnp.sum(onehot * counts[None, :], axis=1))
        weight = TOKENS / (group_sizes[selected_index] * owned)
        placement_index = slot_index(column)
        features = unblock(student_feats[placement_index], widths[selected_index])
        grad_head, gain_gradient, row_gradient, loss = student_pass(features, gain_list[selected_index], heads[selected_index], target, weight)
        token_gradient = token_gradient.at[placement_index].set(regroup_blocks(row_gradient))
        head_grads.append(grad_head)
        gain_grads.append(gain_gradient)
        loss_list.append(loss)
    losses = jnp.stack(loss_list).astype(jnp.float32)
    return (head_grads[0], head_grads[1], head_grads[2], gain_grads[0], gain_grads[1], gain_grads[2], token_gradient, losses)
```

```python
import math

import jax
import jax.numpy as jnp
from jax import lax
from jax.sharding import Mesh
from jax.sharding import PartitionSpec as P

D = 4096
TOKENS = 8192
ROWS = 128
SHARDS = 64
CAP = 14
SLOT = 16
GROUPS = (12, 20, 32)
WIDTHS = (384, 768, 1024)
OFFSETS = (512, 256, 0)
PADDED = (128, 256, 256)
BLOCK = 640
ROOT = math.sqrt(TOKENS)
F32 = jnp.float32
BF16 = jnp.bfloat16
SWAP = [(0, 1), (1, 0)]


def shifted(value, axis, step):
    return lax.ppermute(value, axis, [(i, (i + step) % 4) for i in range(4)])


def gather4(value, axis):
    pos = lax.axis_index(axis)
    out = jnp.zeros((4,) + value.shape, value.dtype)
    parts = [value] + [shifted(value, axis, step) for step in (1, 2, 3)]
    for step in range(4):
        out = lax.dynamic_update_index_in_dim(out, parts[step], (pos + 4 - step) % 4, 0)
    return out


def reduce4(blocks, axis):
    pos = lax.axis_index(axis)
    total = lax.dynamic_index_in_dim(blocks, pos, 0, keepdims=False).astype(F32)
    for step in (1, 2, 3):
        part = lax.dynamic_index_in_dim(blocks, (pos + step) % 4, 0, keepdims=False)
        total = total + shifted(part.astype(BF16), axis, step).astype(F32)
    return total


def gather2(value, axis):
    pos = lax.axis_index(axis)
    other = lax.ppermute(value, axis, SWAP)
    first = jnp.where(pos == 0, value, other)
    second = jnp.where(pos == 0, other, value)
    return jnp.stack([first, second])


def sum2(value, axis):
    return value + lax.ppermute(value, axis, SWAP)


def pick(value, index, axis):
    return lax.dynamic_index_in_dim(value, index, axis, keepdims=False)


def pad_head(head, index):
    quarter = WIDTHS[index] // 4
    blocks = head.reshape(4, quarter, head.shape[1])
    blocks = jnp.pad(blocks, ((0, 0), (0, PADDED[index] - quarter), (0, 0)))
    return blocks.reshape(4 * PADDED[index], head.shape[1])


def pad_gain(gain, index):
    quarter = WIDTHS[index] // 4
    return jnp.pad(gain.reshape(4, quarter), ((0, 0), (0, PADDED[index] - quarter)))


def teacher_sum(attn_out, out_proj):
    y = lax.axis_index("y")
    zh = lax.axis_index("zh")
    c = lax.axis_index("c")
    weights = gather4(out_proj.T, "zl").reshape(256, 1024)
    weights = gather4(weights, "x").reshape(1024, 1024)
    rows = gather4(attn_out, "y").reshape(512, 1024)
    partial = lax.dot_general(rows, weights, (((1,), (1,)), ((), ())), preferred_element_type=F32)
    partial = partial.reshape(2, 2, ROWS, 1024)
    mine = pick(partial, c, 1)
    other = pick(partial, 1 - c, 1).astype(BF16)
    pair = (mine + lax.ppermute(other, "c", SWAP).astype(F32)).astype(BF16)
    total = None
    for k in range(2):
        links = []
        for py in range(4):
            for pzh in range(2):
                for pc in range(2):
                    links.append(((py * 2 + pzh) * 2 + pc, (pc + 2 * ((pzh + k) % 2)) * 4 + py))
        part = lax.ppermute(pick(pair, (zh + k) % 2, 0), ("y", "zh", "c"), links).astype(F32)
        total = part if total is None else total + part
    return total


def per_device(
    attn_out,
    out_proj,
    residual,
    teacher_gain,
    student_feats,
    head_small,
    head_base,
    head_large,
    gain_small,
    gain_base,
    gain_large,
    row_shard,
):
    zh = lax.axis_index("zh")
    c = lax.axis_index("c")
    tensor = zh * 2 + c
    heads = [pad_head(h, i) for i, h in enumerate((head_small, head_base, head_large))]
    gains = [pad_gain(g, i) for i, g in enumerate((gain_small, gain_base, gain_large))]

    shard_ids = jnp.arange(SHARDS, dtype=jnp.int32)
    lower = jnp.arange(ROWS)[:, None] > jnp.arange(ROWS)[None, :]
    slot_ids = jnp.arange(SHARDS * SLOT, dtype=jnp.int32)
    onehots, selectors = [], []
    for i in range(3):
        column = row_shard[:, i]
        onehots.append((column[:, None] == shard_ids[None, :]).astype(F32))
        same = (column[:, None] == column[None, :]) & lower
        rank = jnp.sum(same.astype(jnp.int32), axis=1)
        place = column * SLOT + rank
        selectors.append((place[:, None] == slot_ids[None, :]).astype(BF16))
    own_counts = jnp.concatenate([jnp.sum(o, axis=0) for o in onehots])

    feats = lax.dynamic_slice(student_feats, (0, tensor * 256), (SHARDS * CAP, 256))
    counts_row = jnp.pad(own_counts.astype(BF16), (0, 64))
    extra = jnp.broadcast_to(counts_row[None, None, :], (SHARDS, 1, 256))
    sent = jnp.concatenate(
        [feats.reshape(SHARDS, CAP, 256), extra, jnp.zeros((SHARDS, 1, 256), BF16)], axis=1
    )
    got = lax.all_to_all(sent, ("y", "x", "zl"), 0, 0, tiled=True)
    counts = jnp.sum(got[:, CAP, :192].astype(F32), axis=0)
    got = got.reshape(SHARDS * SLOT, 256)
    parts = [None] * 3
    for i in range(3):
        block = jnp.dot(selectors[i], got, preferred_element_type=F32).astype(BF16)
        quarter = WIDTHS[i] // 4
        parts[i] = jnp.pad(block[:, :quarter], ((0, 0), (0, PADDED[i] - quarter)))
    block = jnp.concatenate([parts[2], parts[1], parts[0]], axis=1)
    blocks = gather2(gather2(block, "c"), "zh").reshape(4, ROWS, BLOCK)

    xhats, normeds, scales, outs, weights = [], [], [], [], []
    for i in range(3):
        x = blocks[:, :, OFFSETS[i] : OFFSETS[i] + PADDED[i]].astype(F32)
        center = jnp.sum(x, axis=(0, 2)) / WIDTHS[i]
        spread = jnp.sum(x * x, axis=(0, 2)) / WIDTHS[i] - center * center
        scale = lax.rsqrt(spread + 1e-06)
        xhat = (x - center[None, :, None]) * scale[None, :, None]
        normed = (xhat * gains[i][:, None, :]).astype(BF16)
        normed = jnp.transpose(normed, (1, 0, 2)).reshape(ROWS, 4 * PADDED[i])
        xhats.append(xhat)
        scales.append(scale)
        normeds.append(normed)
        outs.append(jnp.dot(normed, heads[i], preferred_element_type=F32))
        owned = jnp.sum(onehots[i] * counts[None, 64 * i : 64 * i + 64], axis=1)
        weights.append(TOKENS / (GROUPS[i] * owned))

    hidden = residual.astype(F32) + teacher_sum(attn_out, out_proj)
    sums = jnp.stack([jnp.sum(hidden, axis=1), jnp.sum(hidden * hidden, axis=1)])
    sums = sum2(sum2(sums, "c"), "zh")
    center = sums[0] / D
    spread = sums[1] / D - center * center
    target = (
        (hidden - center[:, None]) * lax.rsqrt(spread + 1e-06)[:, None] * teacher_gain
    ).astype(BF16).astype(F32)

    grads, backs, moments = [], [], []
    for i in range(3):
        diff = outs[i] - target
        error = (weights[i][:, None] * diff).astype(BF16)
        grad = lax.dot_general(normeds[i], error, (((0,), (0,)), ((), ())), preferred_element_type=F32)
        grad = (grad / ROOT).astype(BF16).reshape(4, PADDED[i], 1024)
        grads.append(grad[:, : WIDTHS[i] // 4])
        back = lax.dot_general(error, heads[i], (((1,), (1,)), ((), ())), preferred_element_type=F32)
        back = jnp.transpose(back.reshape(ROWS, 4, PADDED[i]), (1, 0, 2))
        backs.append(back)
        upper = back * gains[i][:, None, :]
        moments.append(jnp.sum(upper, axis=(0, 2)))
        moments.append(jnp.sum(upper * xhats[i], axis=(0, 2)))
        moments.append(weights[i] * jnp.sum(diff * diff, axis=1))

    back = jnp.concatenate([backs[2], backs[1], backs[0]], axis=2).reshape(2, 2, ROWS, BLOCK)
    back = pick(back, c, 1) + lax.ppermute(pick(back, 1 - c, 1).astype(BF16), "c", SWAP).astype(F32)
    back = pick(back, zh, 0) + lax.ppermute(pick(back, 1 - zh, 0).astype(BF16), "zh", SWAP).astype(F32)
    moments = sum2(sum2(jnp.stack(moments), "c"), "zh")

    slots = jnp.zeros((SHARDS * SLOT, 256), F32)
    gain_parts = []
    for i in range(3):
        quarter = WIDTHS[i] // 4
        mine = back[:, OFFSETS[i] : OFFSETS[i] + PADDED[i]]
        xhat = pick(xhats[i], tensor, 0)
        upper = mine * pick(gains[i], tensor, 0)[None, :]
        first = moments[3 * i][:, None] / WIDTHS[i]
        second = moments[3 * i + 1][:, None] / WIDTHS[i]
        rows = scales[i][:, None] * (upper - first - xhat * second)
        rows = jnp.pad(rows[:, :quarter], ((0, 0), (0, 256 - quarter))).astype(BF16)
        slots = slots + lax.dot_general(
            selectors[i], rows, (((0,), (0,)), ((), ())), preferred_element_type=F32
        )
        gain_parts.append(jnp.sum(mine * xhat, axis=0)[:quarter] / ROOT)
    slots = slots.astype(BF16).reshape(SHARDS, SLOT, 256)
    token_gradient = lax.all_to_all(slots, ("y", "x", "zl"), 0, 0, tiled=True)
    token_gradient = token_gradient[:, :CAP].reshape(SHARDS * CAP, 256)

    tree = jnp.concatenate([grads[2], grads[1], grads[0]], axis=1)
    tree = reduce4(tree, "y")
    edges = (0, 256, 448, 544)
    for axis in ("x", "zl"):
        tree = jnp.concatenate(
            [tree[edges[j] : edges[j + 1]].reshape(4, -1, 1024) for j in range(3)], axis=1
        )
        tree = reduce4(tree, axis)
        edges = tuple(e // 4 for e in edges)

    losses = jnp.stack([jnp.sum(moments[3 * i + 2]) for i in range(3)]) / (2.0 * D * TOKENS)
    small = jnp.concatenate(gain_parts + [losses, jnp.zeros((1024 - 547,), F32)]).reshape(8, 128)
    for axis in ("y", "x", "zl"):
        small = small + shifted(small, axis, 1) + shifted(small, axis, 2) + shifted(small, axis, 3)
    small = small.reshape(1024)
    return (
        tree[28:34],
        tree[16:28],
        tree[0:16],
        small[0:96],
        small[96:288],
        small[288:544],
        token_gradient,
        small[544:547],
    )


def solution(mesh):
    fine = Mesh(mesh.devices.reshape(4, 4, 4, 2, 2), ("y", "x", "zl", "zh", "c"))
    dp = ("y", "x", "zl")
    tp = ("zh", "c")
    return jax.shard_map(
        per_device,
        mesh=fine,
        in_specs=(
            P(dp, tp),
            P(tp, dp),
            P(dp, tp),
            P(tp),
            P(dp, None),
            P(None, tp),
            P(None, tp),
            P(None, tp),
            P(),
            P(),
            P(),
            P(dp, None),
        ),
        out_specs=(
            P(dp, tp),
            P(dp, tp),
            P(dp, tp),
            P(tp),
            P(tp),
            P(tp),
            P(dp, tp),
            P(),
        ),
        check_vma=False,
    )
```

```python
import functools
import math

import jax
import jax.numpy as jnp
from jax import lax
from jax.experimental import pallas as pl
from jax.experimental.pallas import tpu as pltpu
from jax.sharding import Mesh
from jax.sharding import PartitionSpec as P

D = 4096
TOKENS = 8192
ROWS = 128
SHARDS = 64
CAP = 14
SLOT = 16
GROUPS = (12, 20, 32)
WIDTHS = (384, 768, 1024)
QUARTERS = (96, 192, 256)
OFFSETS = (512, 256, 0)
BLOCK = 640
SPARE = 448
ROOT = math.sqrt(TOKENS)
F32 = jnp.float32
BF16 = jnp.bfloat16
SWAP = [(0, 1), (1, 0)]
VMEM_LIMIT = 48 * 1024 * 1024


def call(body, outs, *args, scratch=(), flops=0, moved=0):
    specs = [pl.BlockSpec(memory_space=pltpu.SMEM)]
    specs += [pl.BlockSpec(memory_space=pltpu.VMEM)] * (len(args) - 1)
    return pl.pallas_call(
        body,
        out_shape=[jax.ShapeDtypeStruct(shape, dtype) for shape, dtype in outs],
        in_specs=specs,
        out_specs=[pl.BlockSpec(memory_space=pltpu.VMEM)] * len(outs),
        scratch_shapes=[pltpu.VMEM(shape, dtype) for shape, dtype in scratch],
        compiler_params=pltpu.CompilerParams(vmem_limit_bytes=VMEM_LIMIT),
        cost_estimate=pl.CostEstimate(flops=flops, bytes_accessed=moved, transcendentals=0),
    )(*args)


def dot(a, b):
    return jnp.dot(a, b, preferred_element_type=F32)


def dot_t(a, b):
    return lax.dot_general(a, b, (((1,), (1,)), ((), ())), preferred_element_type=F32)


def shifted(value, axis, step):
    return lax.ppermute(value, axis, [(i, (i + step) % 4) for i in range(4)])


def swapped(value, axis):
    return lax.ppermute(value, axis, SWAP)


def split_sum(value):
    high = value.astype(BF16)
    return high, (value - high.astype(F32)).astype(BF16)


Y, X, ZL, ZH, C = range(5)


def teacher_kernel(pos, a0, a1, a2, a3, w0, w1, w2, w3, mine, other, rows, weights):
    y, x, zl, c = pos[Y], pos[X], pos[ZL], pos[C]
    for step, part in enumerate((a0, a1, a2, a3)):
        rows[lax.rem(y + 4 - step, 4)] = part[...]
    for step, part in enumerate((w0, w1, w2, w3)):
        first = lax.rem(x + 4 - step, 4) * 256
        for turn in range(4):
            start = pl.multiple_of(first + lax.rem(zl + 4 - turn, 4) * 64, 64)
            weights[pl.ds(start, 64), :] = part[turn * 64 : turn * 64 + 64, :]
    for half in range(2):
        mine[half] = dot_t(rows[c + 2 * half], weights[...])
        other[half] = dot_t(rows[1 - c + 2 * half], weights[...]).astype(BF16)


def pair_kernel(pos, mine, got, first, second):
    zh = pos[ZH]
    first[...] = (mine[zh] + got[zh].astype(F32)).astype(BF16)
    second[...] = (mine[1 - zh] + got[1 - zh].astype(F32)).astype(BF16)


def hidden_kernel(pos, first, second, residual, hidden, sums):
    value = residual[...].astype(F32) + (first[...].astype(F32) + second[...].astype(F32))
    hidden[...] = value
    lane = lax.broadcasted_iota(jnp.int32, (ROWS, 128), 1)
    total = jnp.sum(value, axis=1, keepdims=True)
    square = jnp.sum(value * value, axis=1, keepdims=True)
    both = jnp.where(lane == 0, total, jnp.where(lane == 1, square, 0.0))
    sums[...] = jnp.transpose(both)[0:8]


def place_kernel(pos, shard, shard_t, got, block, place_t, weights):
    token = lax.broadcasted_iota(jnp.int32, (ROWS, ROWS), 0)
    token_t = lax.broadcasted_iota(jnp.int32, (ROWS, ROWS), 1)
    slot = lax.broadcasted_iota(jnp.int32, (ROWS, SHARDS * SLOT), 1)
    spare = lax.broadcasted_iota(jnp.int32, (8, SHARDS * SLOT), 1)
    lane = lax.broadcasted_iota(jnp.int32, (ROWS, 256), 1)
    counts = dot((lax.rem(spare, SLOT) == CAP).astype(F32).astype(BF16), got[...])[0:1]
    block[...] = jnp.zeros_like(block)
    place_t[...] = jnp.zeros_like(place_t)
    for i in range(3):
        column = shard[:, i : i + 1]
        row = shard_t[i : i + 1, :]
        same = column == row
        rank = jnp.sum(jnp.where(same & (token_t < token), 1, 0), axis=1, keepdims=True)
        rank_t = jnp.sum(jnp.where(same & (token < token_t), 1, 0), axis=0, keepdims=True)
        place_t[i : i + 1, :] = row * SLOT + rank_t
        select = (slot == column * SLOT + rank).astype(F32).astype(BF16)
        value = dot(select, got[...]).astype(BF16)
        block[:, OFFSETS[i] : OFFSETS[i] + QUARTERS[i]] = value[:, : QUARTERS[i]]
        owned = jnp.sum(jnp.where(lane == column + 64 * i, counts, 0.0), axis=1, keepdims=True)
        weights[:, 128 * i : 128 * i + 128] = jnp.broadcast_to(
            TOKENS / (GROUPS[i] * owned), (ROWS, 128)
        )


def student_kernel(
    pos, own, own_c, own_z, own_zc, gain_s, gain_b, gain_l, head_s, head_b, head_l,
    xhat, scales, lines_l, lines_x, outs, blocks, lines_s,
):
    zh, c = pos[ZH], pos[C]
    blocks[2 * zh + c] = own[...]
    blocks[2 * zh + 1 - c] = own_c[...]
    blocks[2 * (1 - zh) + c] = own_z[...]
    blocks[2 * (1 - zh) + 1 - c] = own_zc[...]
    xhat[...] = jnp.zeros_like(xhat)
    for i, (gain, head) in enumerate(((gain_s, head_s), (gain_b, head_b), (gain_l, head_l))):
        wide, first = QUARTERS[i], OFFSETS[i]
        parts = [blocks[b, :, first : first + wide].astype(F32) for b in range(4)]
        total = sum(jnp.sum(p, axis=1, keepdims=True) for p in parts)
        square = sum(jnp.sum(p * p, axis=1, keepdims=True) for p in parts)
        center = total / WIDTHS[i]
        scale = lax.rsqrt(square / WIDTHS[i] - center * center + 1e-06)
        scales[:, 128 * i : 128 * i + 128] = jnp.broadcast_to(scale, (ROWS, 128))
        out = jnp.zeros((ROWS, 1024), F32)
        for b in range(4):
            value = (parts[b] - center) * scale
            xhat[b, :, first : first + wide] = value
            normed = value * gain[:, b * wide : b * wide + wide]
            out = out + dot(normed.astype(BF16), head[b * wide : b * wide + wide, :])
            lines = jnp.transpose(normed)
            if i == 2:
                lines_l[b] = lines.astype(BF16)
            elif i == 1:
                for x in range(4):
                    lines_x[x, b * 48 : b * 48 + 48, :] = lines[x * 48 : x * 48 + 48].astype(BF16)
            else:
                for x in range(4):
                    lines_s[x, b * 24 : b * 24 + 24, :] = lines[x * 24 : x * 24 + 24]
        outs[i] = out
    lines_x[:, 192:288, :] = lines_s[...].astype(BF16)


def error_kernel(
    pos, hidden, sums, teacher_gain, outs, weights, lines_l, lines_x, xhat,
    gain_s, gain_b, gain_l, head_s, head_b, head_l,
    l0, l1, l2, l3, x0, x1, x2, x3, mine, other, backs, extra,
):
    y, x, c = pos[Y], pos[X], pos[C]
    stats = jnp.transpose(jnp.concatenate([sums[...], jnp.zeros((120, 128), F32)], axis=0))
    center = stats[:, 0:1] / D
    spread = stats[:, 1:2] / D - center * center
    target = (hidden[...] - center) * lax.rsqrt(spread + 1e-06) * teacher_gain[...]
    target = target.astype(BF16).astype(F32)
    lane = lax.broadcasted_iota(jnp.int32, (ROWS, 64), 1)
    moments = jnp.zeros((ROWS, 64), F32)
    extra[...] = jnp.zeros_like(extra)
    errors = []
    for i, (gain, head) in enumerate(((gain_s, head_s), (gain_b, head_b), (gain_l, head_l))):
        wide, first = QUARTERS[i], OFFSETS[i]
        weight = weights[:, 128 * i : 128 * i + 1]
        diff = outs[i] - target
        error = (weight * diff).astype(BF16)
        errors.append(error)
        loss = jnp.sum(weight * jnp.sum(diff * diff, axis=1, keepdims=True), axis=0, keepdims=True)
        extra[0:1, BLOCK + 128 * i : BLOCK + 128 * i + 128] = jnp.broadcast_to(loss, (1, 128))
        one = jnp.zeros((ROWS, 1), F32)
        two = jnp.zeros((ROWS, 1), F32)
        for b in range(4):
            back = dot_t(error, head[b * wide : b * wide + wide, :])
            value = xhat[b, :, first : first + wide]
            upper = back * gain[:, b * wide : b * wide + wide]
            one = one + jnp.sum(upper, axis=1, keepdims=True)
            two = two + jnp.sum(upper * value, axis=1, keepdims=True)
            backs[b, :, first : first + wide] = back
            extra[b : b + 1, first : first + wide] = jnp.sum(back * value, axis=0, keepdims=True)
        moments = jnp.where(lane == 2 * i, one, jnp.where(lane == 2 * i + 1, two, moments))
    high, low = split_sum(moments)
    turned = jnp.concatenate([high.astype(F32)[:, :32], low.astype(F32)[:, :32]], axis=1)
    zeros = jnp.zeros((ROWS, 32), F32)
    for half in range(2):
        mine[half] = backs[2 * half + c]
        mine[half, :, SPARE : SPARE + 64] = moments
        mine[half, :, BLOCK - 32 : BLOCK] = zeros
        other[half] = backs[2 * half + 1 - c].astype(BF16)
        other[half, :, SPARE : SPARE + 64] = turned.astype(BF16)
        other[half, :, BLOCK - 32 : BLOCK] = zeros.astype(BF16)
    high, low = split_sum(extra[...])
    for step, out in enumerate((l0, l1, l2, l3)):
        out[0:256, :] = dot(lines_l[lax.rem(y + step, 4)], errors[2]).astype(BF16)
        out[256:272, :] = jnp.concatenate([high, low], axis=0)
    for step, out in enumerate((x0, x1, x2, x3)):
        index = lax.rem(x + step, 4)
        out[0:192, :] = dot(lines_x[index, 0:192, :], errors[1]).astype(BF16)
        out[192:288, :] = dot(lines_x[index, 192:288, :], errors[0]).astype(BF16)


def back_kernel(pos, mine, got, keep, send, both):
    zh = pos[ZH]
    for half in range(2):
        both[half] = mine[half] + got[half].astype(F32)
    keep[...] = both[zh]
    send[...] = both[1 - zh].astype(BF16)
    value = both[0, :, SPARE : SPARE + 64]
    moments = value[:, 0:32] + value[:, 32:64]
    high, low = split_sum(moments)
    keep[:, SPARE : SPARE + 64] = jnp.concatenate([moments, jnp.zeros((ROWS, 32), F32)], axis=1)
    send[:, SPARE : SPARE + 64] = jnp.concatenate(
        [high.astype(F32), low.astype(F32)], axis=1
    ).astype(BF16)


def rows_kernel(pos, keep, got, xhat, scales, place_t, gain_s, gain_b, gain_l, slots, gains):
    t = 2 * pos[ZH] + pos[C]
    back = keep[...] + got[...].astype(F32)
    moments = back[:, SPARE : SPARE + 32] + back[:, SPARE + 32 : SPARE + 64]
    value = xhat[t]
    for i, gain in enumerate((gain_s, gain_b, gain_l)):
        wide = QUARTERS[i]
        for b in range(4):
            gains[b : b + 1, OFFSETS[i] : OFFSETS[i] + wide] = gain[:, b * wide : b * wide + wide]
    gain_row = gains[pl.ds(t, 1), :]
    slot = lax.broadcasted_iota(jnp.int32, (SHARDS * SLOT, ROWS), 0)
    total = jnp.zeros((SHARDS * SLOT, 256), F32)
    for i in range(3):
        first, wide = OFFSETS[i], QUARTERS[i]
        hat = value[:, first : first + wide]
        upper = back[:, first : first + wide] * gain_row[:, first : first + wide]
        one = moments[:, 2 * i : 2 * i + 1] / WIDTHS[i]
        two = moments[:, 2 * i + 1 : 2 * i + 2] / WIDTHS[i]
        rows = scales[:, 128 * i : 128 * i + 1] * (upper - one - hat * two)
        if wide < 256:
            rows = jnp.concatenate([rows, jnp.zeros((ROWS, 256 - wide), F32)], axis=1)
        select = (slot == place_t[i : i + 1, :]).astype(F32).astype(BF16)
        total = total + dot(select, rows.astype(BF16))
    slots[...] = total.astype(BF16)


def large_kernel(pos, p0, p1, p2, p3, keep, m1, m2, m3, total):
    x = pos[X]
    total[...] = sum(p[...].astype(F32) for p in (p0, p1, p2, p3))
    pieces = total[256:264, :] + total[264:272, :]
    high, low = split_sum(pieces)
    keep[0:64, :] = total[pl.ds(pl.multiple_of(x * 64, 64), 64), :]
    keep[64:72, :] = pieces
    for step, out in ((1, m1), (2, m2), (3, m3)):
        start = pl.multiple_of(lax.rem(x + step, 4) * 64, 64)
        out[0:64, :] = total[pl.ds(start, 64), :].astype(BF16)
        out[64:80, :] = jnp.concatenate([high, low], axis=0)


def mixed_kernel(pos, p0, p1, p2, p3, keep, m1, m2, m3, total):
    y = pos[Y]
    total[...] = sum(p[...].astype(F32) for p in (p0, p1, p2, p3))
    keep[0:48, :] = total[pl.ds(pl.multiple_of(y * 48, 8), 48), :]
    keep[48:72, :] = total[pl.ds(pl.multiple_of(192 + y * 24, 8), 24), :]
    for step, out in ((1, m1), (2, m2), (3, m3)):
        index = lax.rem(y + step, 4)
        out[0:48, :] = total[pl.ds(pl.multiple_of(index * 48, 8), 48), :].astype(BF16)
        small = total[pl.ds(pl.multiple_of(192 + index * 24, 8), 24), :]
        out[48:80, :] = jnp.concatenate([small, jnp.zeros((8, 1024), F32)], axis=0).astype(BF16)


def third_kernel(pos, kl, l1, l2, l3, kx, x1, x2, x3, keep, m1, m2, m3, parts):
    zl = pos[ZL]
    large = kl[0:64, :] + sum(p[0:64, :].astype(F32) for p in (l1, l2, l3))
    pieces = kl[64:72, :] + sum(
        p[64:80, :].astype(F32)[0:8] + p[64:80, :].astype(F32)[8:16] for p in (l1, l2, l3)
    )
    mixed = kx[...] + sum(p[...].astype(F32)[0:72] for p in (x1, x2, x3))
    high, low = split_sum(pieces)
    for i in range(4):
        parts[i, 0:16, :] = large[16 * i : 16 * i + 16]
        parts[i, 16:28, :] = mixed[12 * i : 12 * i + 12]
        parts[i, 28:34, :] = mixed[48 + 6 * i : 48 + 6 * i + 6]
        parts[i, 34:48, :] = jnp.zeros((14, 1024), F32)
    keep[0:48, :] = parts[zl]
    keep[48:56, :] = pieces
    for step, out in ((1, m1), (2, m2), (3, m3)):
        out[0:48, :] = parts[lax.rem(zl + step, 4)].astype(BF16)
        out[48:64, :] = jnp.concatenate([high, low], axis=0)


def last_kernel(pos, keep, m1, m2, m3, small, base, large, pieces):
    total = keep[0:48, :] + sum(p[0:48, :].astype(F32) for p in (m1, m2, m3))
    total = total / ROOT
    large[...] = total[0:16]
    base[...] = total[16:28]
    small[...] = total[28:34]
    pieces[...] = keep[48:56, :] + sum(
        p[48:64, :].astype(F32)[0:8] + p[48:64, :].astype(F32)[8:16] for p in (m1, m2, m3)
    )


def per_device(
    attn_out,
    out_proj,
    residual,
    teacher_gain,
    student_feats,
    head_small,
    head_base,
    head_large,
    gain_small,
    gain_base,
    gain_large,
    row_shard,
):
    pos = jnp.stack([lax.axis_index(a).astype(jnp.int32) for a in ("y", "x", "zl", "zh", "c")])
    tensor = 2 * pos[ZH] + pos[C]
    heads = (head_small, head_base, head_large)
    gains = (gain_small[None, :], gain_base[None, :], gain_large[None, :])

    own = out_proj.T
    weights = jnp.concatenate([own] + [shifted(own, "zl", s) for s in (1, 2, 3)], axis=0)
    rows = [attn_out] + [shifted(attn_out, "y", s) for s in (1, 2, 3)]
    weights = [weights] + [shifted(weights, "x", s) for s in (1, 2, 3)]

    shard_t = jnp.pad(row_shard.T, ((0, 5), (0, 0)))
    shard_ids = jnp.arange(SHARDS, dtype=jnp.int32)
    named = (row_shard.T[:, :, None] == shard_ids[None, None, :]).astype(F32)
    own_counts = jnp.sum(named, axis=1).reshape(3 * SHARDS)
    feats = lax.dynamic_slice(student_feats, (0, tensor * 256), (SHARDS * CAP, 256))
    counts_row = jnp.pad(own_counts.astype(BF16), (0, 64))
    ride = jnp.broadcast_to(counts_row[None, None, :], (SHARDS, 2, 256))
    sent = jnp.concatenate([feats.reshape(SHARDS, CAP, 256), ride], axis=1)
    got = lax.all_to_all(sent, ("y", "x", "zl"), 0, 0, tiled=True).reshape(SHARDS * SLOT, 256)
    block, place_t, token_weights = call(
        place_kernel,
        [((ROWS, BLOCK), BF16), ((8, ROWS), jnp.int32), ((ROWS, 384), F32)],
        pos, row_shard, shard_t, got,
        flops=3 * 2 * 128 * 1024 * 256, moved=1 << 20,
    )
    block_c = swapped(block, "c")
    block_z = swapped(block, "zh")
    block_zc = swapped(block_z, "c")

    mine, other = call(
        teacher_kernel,
        [((2, ROWS, 1024), F32), ((2, ROWS, 1024), BF16)],
        pos, *rows, *weights,
        scratch=[((4, ROWS, 1024), BF16), ((1024, 1024), BF16)],
        flops=2 * 512 * 1024 * 1024, moved=5 << 20,
    )
    first, second = call(
        pair_kernel, [((ROWS, 1024), BF16)] * 2, pos, mine, swapped(other, "c"), moved=2 << 20
    )
    parts = []
    for k, value in enumerate((first, second)):
        links = []
        for py in range(4):
            for pzh in range(2):
                for pc in range(2):
                    links.append(((py * 2 + pzh) * 2 + pc, (pc + 2 * ((pzh + k) % 2)) * 4 + py))
        parts.append(lax.ppermute(value, ("y", "zh", "c"), links))

    xhat, scales, lines_l, lines_x, outs = call(
        student_kernel,
        [
            ((4, ROWS, BLOCK), F32),
            ((ROWS, 384), F32),
            ((4, 256, ROWS), BF16),
            ((4, 288, ROWS), BF16),
            ((3, ROWS, 1024), F32),
        ],
        pos, block, block_c, block_z, block_zc, *gains, *heads,
        scratch=[((4, ROWS, BLOCK), BF16), ((4, 96, ROWS), F32)],
        flops=2 * 128 * 2176 * 1024, moved=9 << 20,
    )
    parts, outs = lax.optimization_barrier((parts, outs))

    hidden, sums = call(
        hidden_kernel, [((ROWS, 1024), F32), ((8, ROWS), F32)], pos, *parts, residual, moved=1 << 20
    )
    sums = sums + swapped(sums, "c")
    sums = sums + swapped(sums, "zh")

    outputs = call(
        error_kernel,
        [((272, 1024), BF16)] * 4
        + [((288, 1024), BF16)] * 4
        + [((2, ROWS, BLOCK), F32), ((2, ROWS, BLOCK), BF16)],
        pos, hidden, sums, teacher_gain[None, :], outs, token_weights, lines_l, lines_x, xhat,
        *gains, *heads,
        scratch=[((4, ROWS, BLOCK), F32), ((8, 1024), F32)],
        flops=4 * 128 * 2176 * 1024, moved=15 << 20,
    )
    large, mixed, (mine, other) = outputs[0:4], outputs[4:8], outputs[8:10]

    keep, send = call(
        back_kernel,
        [((ROWS, BLOCK), F32), ((ROWS, BLOCK), BF16)],
        pos, mine, swapped(other, "c"),
        scratch=[((2, ROWS, BLOCK), F32)], moved=2 << 20,
    )
    (slots,) = call(
        rows_kernel,
        [((SHARDS * SLOT, 256), BF16)],
        pos, keep, swapped(send, "zh"), xhat, scales, place_t, *gains,
        scratch=[((8, BLOCK), F32)],
        flops=3 * 2 * 128 * 1024 * 256, moved=2 << 20,
    )
    token_gradient = lax.all_to_all(
        slots.reshape(SHARDS, SLOT, 256), ("y", "x", "zl"), 0, 0, tiled=True
    )
    token_gradient = token_gradient[:, :CAP].reshape(SHARDS * CAP, 256)

    keep_l, *sent_l = call(
        large_kernel,
        [((72, 1024), F32)] + [((80, 1024), BF16)] * 3,
        pos, large[0], *[shifted(large[s], "y", s) for s in (1, 2, 3)],
        scratch=[((272, 1024), F32)], moved=4 << 20,
    )
    keep_x, *sent_x = call(
        mixed_kernel,
        [((72, 1024), F32)] + [((80, 1024), BF16)] * 3,
        pos, mixed[0], *[shifted(mixed[s], "x", s) for s in (1, 2, 3)],
        scratch=[((288, 1024), F32)], moved=4 << 20,
    )
    keep, *sent = call(
        third_kernel,
        [((56, 1024), F32)] + [((64, 1024), BF16)] * 3,
        pos,
        keep_l, *[shifted(sent_l[s - 1], "x", s) for s in (1, 2, 3)],
        keep_x, *[shifted(sent_x[s - 1], "y", s) for s in (1, 2, 3)],
        scratch=[((4, 48, 1024), F32)], moved=2 << 20,
    )
    grad_small, grad_base, grad_large, pieces = call(
        last_kernel,
        [((6, 1024), F32), ((12, 1024), F32), ((16, 1024), F32), ((8, 1024), F32)],
        pos, keep, *[shifted(sent[s - 1], "zl", s) for s in (1, 2, 3)],
        moved=1 << 20,
    )

    pieces = pieces + swapped(pieces, "c")
    pieces = pieces + swapped(pieces, "zh")
    row = lax.dynamic_index_in_dim(pieces, tensor, 0, keepdims=False) / ROOT
    losses = jnp.stack([pieces[0, BLOCK + 128 * i] for i in range(3)]) / (2.0 * D * TOKENS)
    return (
        grad_small,
        grad_base,
        grad_large,
        row[OFFSETS[0] : OFFSETS[0] + 96],
        row[OFFSETS[1] : OFFSETS[1] + 192],
        row[OFFSETS[2] : OFFSETS[2] + 256],
        token_gradient,
        losses,
    )


def solution(mesh):
    fine = Mesh(mesh.devices.reshape(4, 4, 4, 2, 2), ("y", "x", "zl", "zh", "c"))
    dp = ("y", "x", "zl")
    tp = ("zh", "c")
    return jax.shard_map(
        per_device,
        mesh=fine,
        in_specs=(
            P(dp, tp),
            P(tp, dp),
            P(dp, tp),
            P(tp),
            P(dp, None),
            P(None, tp),
            P(None, tp),
            P(None, tp),
            P(),
            P(),
            P(),
            P(dp, None),
        ),
        out_specs=(
            P(dp, tp),
            P(dp, tp),
            P(dp, tp),
            P(tp),
            P(tp),
            P(tp),
            P(dp, tp),
            P(),
        ),
        check_vma=False,
    )
```

```python
import functools
import math

import jax
import jax.numpy as jnp
from jax import lax
from jax.experimental import pallas as pl
from jax.experimental.pallas import tpu as pltpu
from jax.sharding import Mesh
from jax.sharding import PartitionSpec as P

D = 4096
TOKENS = 8192
ROWS = 128
SHARDS = 64
CAP = 14
SLOT = 16
GROUPS = (12, 20, 32)
WIDTHS = (384, 768, 1024)
QUARTERS = (96, 192, 256)
OFFSETS = (512, 256, 0)
BLOCK = 640
LINES = (448, 256, 0)
SPARE = 448
ROOT = math.sqrt(TOKENS)
F32 = jnp.float32
BF16 = jnp.bfloat16
SWAP = [(0, 1), (1, 0)]
MIB = 1024 * 1024


def call(body, outs, *args, scratch=(), flops=0, moved=0, room=8):
    specs = [pl.BlockSpec(memory_space=pltpu.SMEM)]
    specs += [pl.BlockSpec(memory_space=pltpu.VMEM)] * (len(args) - 1)
    return pl.pallas_call(
        body,
        out_shape=[jax.ShapeDtypeStruct(shape, dtype) for shape, dtype in outs],
        in_specs=specs,
        out_specs=[pl.BlockSpec(memory_space=pltpu.VMEM)] * len(outs),
        scratch_shapes=[pltpu.VMEM(shape, dtype) for shape, dtype in scratch],
        compiler_params=pltpu.CompilerParams(vmem_limit_bytes=room * MIB),
        cost_estimate=pl.CostEstimate(flops=flops, bytes_accessed=moved, transcendentals=0),
    )(*args)


def dot(a, b):
    return jnp.dot(a, b, preferred_element_type=F32)


def dot_t(a, b):
    return lax.dot_general(a, b, (((1,), (1,)), ((), ())), preferred_element_type=F32)


def shifted(value, axis, step):
    return lax.ppermute(value, axis, [(i, (i + step) % 4) for i in range(4)])


def swapped(value, axis):
    return lax.ppermute(value, axis, SWAP)


def split_sum(value):
    high = value.astype(BF16)
    return high, (value - high.astype(F32)).astype(BF16)


Y, X, ZL, ZH, C = range(5)


def teacher_kernel(pos, a0, a1, a2, a3, w0, w1, w2, w3, mine, other, rows, weights):
    y, x, zl, c = pos[Y], pos[X], pos[ZL], pos[C]
    for step, part in enumerate((a0, a1, a2, a3)):
        index = lax.rem(y + 4 - step, 4)
        place = 2 * lax.rem(index + c, 2) + lax.div(index, 2)
        rows[pl.ds(pl.multiple_of(place * ROWS, ROWS), ROWS), :] = part[...]
    for step, part in enumerate((w0, w1, w2, w3)):
        first = lax.rem(x + 4 - step, 4) * 256
        for turn in range(4):
            start = pl.multiple_of(first + lax.rem(zl + 4 - turn, 4) * 64, 64)
            weights[pl.ds(start, 64), :] = part[turn * 64 : turn * 64 + 64, :]
    product = dot_t(rows[...], weights[...]).astype(BF16)
    for half in range(2):
        mine[half] = product[half * ROWS : half * ROWS + ROWS]
        other[half] = product[(half + 2) * ROWS : (half + 3) * ROWS]


def pair_kernel(pos, mine, got, first, second):
    zh = pos[ZH]
    first[...] = (mine[zh].astype(F32) + got[zh].astype(F32)).astype(BF16)
    second[...] = (mine[1 - zh].astype(F32) + got[1 - zh].astype(F32)).astype(BF16)


def hidden_kernel(pos, first, second, residual, hidden, sums):
    value = residual[...].astype(F32) + (first[...].astype(F32) + second[...].astype(F32))
    hidden[...] = value
    lane = lax.broadcasted_iota(jnp.int32, (ROWS, 128), 1)
    total = jnp.sum(value, axis=1, keepdims=True)
    square = jnp.sum(value * value, axis=1, keepdims=True)
    both = jnp.where(lane == 0, total, jnp.where(lane == 1, square, 0.0))
    sums[...] = jnp.transpose(both)[0:8]


def place_kernel(pos, shard, shard_t, got, block, place_t, weights):
    token = lax.broadcasted_iota(jnp.int32, (ROWS, ROWS), 0)
    token_t = lax.broadcasted_iota(jnp.int32, (ROWS, ROWS), 1)
    slot = lax.broadcasted_iota(jnp.int32, (ROWS, SHARDS * SLOT), 1)
    spare = lax.broadcasted_iota(jnp.int32, (8, SHARDS * SLOT), 1)
    lane = lax.broadcasted_iota(jnp.int32, (ROWS, 256), 1)
    counts = dot((lax.rem(spare, SLOT) == CAP).astype(F32).astype(BF16), got[...])[0:1]
    block[...] = jnp.zeros_like(block)
    place_t[...] = jnp.zeros_like(place_t)
    for i in range(3):
        column = shard[:, i : i + 1]
        row = shard_t[i : i + 1, :]
        same = column == row
        rank = jnp.sum(jnp.where(same & (token_t < token), 1, 0), axis=1, keepdims=True)
        rank_t = jnp.sum(jnp.where(same & (token < token_t), 1, 0), axis=0, keepdims=True)
        place_t[i : i + 1, :] = row * SLOT + rank_t
        select = (slot == column * SLOT + rank).astype(F32).astype(BF16)
        value = dot(select, got[...]).astype(BF16)
        block[:, OFFSETS[i] : OFFSETS[i] + QUARTERS[i]] = value[:, : QUARTERS[i]]
        owned = jnp.sum(jnp.where(lane == column + 64 * i, counts, 0.0), axis=1, keepdims=True)
        weights[:, 128 * i : 128 * i + 128] = jnp.broadcast_to(
            TOKENS / (GROUPS[i] * owned), (ROWS, 128)
        )


def student_kernel(
    pos, own, own_c, own_z, own_zc, gain_s, gain_b, gain_l, head_s, head_b, head_l,
    xhat, scales, outs, n0, n1, n2, n3, blocks, lines,
):
    y, zh, c = pos[Y], pos[ZH], pos[C]
    blocks[2 * zh + c] = own[...]
    blocks[2 * zh + 1 - c] = own_c[...]
    blocks[2 * (1 - zh) + c] = own_z[...]
    blocks[2 * (1 - zh) + 1 - c] = own_zc[...]
    xhat[...] = jnp.zeros_like(xhat)
    for i, (gain, head) in enumerate(((gain_s, head_s), (gain_b, head_b), (gain_l, head_l))):
        wide, first, first_line = QUARTERS[i], OFFSETS[i], LINES[i]
        parts = [blocks[b, :, first : first + wide].astype(F32) for b in range(4)]
        total = sum(jnp.sum(p, axis=1, keepdims=True) for p in parts)
        square = sum(jnp.sum(p * p, axis=1, keepdims=True) for p in parts)
        center = total / WIDTHS[i]
        scale = lax.rsqrt(square / WIDTHS[i] - center * center + 1e-06)
        scales[:, 128 * i : 128 * i + 128] = jnp.broadcast_to(scale, (ROWS, 128))
        out = jnp.zeros((ROWS, 1024), F32)
        for b in range(4):
            value = (parts[b] - center) * scale
            xhat[b, :, first : first + wide] = value
            normed = value * gain[:, b * wide : b * wide + wide]
            out = out + dot(normed.astype(BF16), head[b * wide : b * wide + wide, :])
            lines[b, first_line : first_line + wide, :] = jnp.transpose(normed).astype(BF16)
        outs[i] = out
    for step, out in enumerate((n0, n1, n2, n3)):
        out[...] = lines[lax.rem(y + step, 4)]


def error_kernel(
    pos, hidden, sums, teacher_gain, outs, weights, xhat,
    gain_s, gain_b, gain_l, head_s, head_b, head_l,
    errors, mine, other, backs,
):
    c = pos[C]
    stats = jnp.transpose(jnp.concatenate([sums[...], jnp.zeros((120, 128), F32)], axis=0))
    center = stats[:, 0:1] / D
    spread = stats[:, 1:2] / D - center * center
    target = (hidden[...] - center) * lax.rsqrt(spread + 1e-06) * teacher_gain[...]
    target = target.astype(BF16).astype(F32)
    lane = lax.broadcasted_iota(jnp.int32, (ROWS, 64), 1)
    moments = jnp.zeros((ROWS, 64), F32)
    for i, (gain, head) in enumerate(((gain_s, head_s), (gain_b, head_b), (gain_l, head_l))):
        wide, first = QUARTERS[i], OFFSETS[i]
        weight = weights[:, 128 * i : 128 * i + 1]
        diff = outs[i] - target
        error = (weight * diff).astype(BF16)
        errors[i] = error
        loss = weight * jnp.sum(diff * diff, axis=1, keepdims=True)
        one = jnp.zeros((ROWS, 1), F32)
        two = jnp.zeros((ROWS, 1), F32)
        for b in range(4):
            back = dot_t(error, head[b * wide : b * wide + wide, :])
            value = xhat[b, :, first : first + wide]
            upper = back * gain[:, b * wide : b * wide + wide]
            one = one + jnp.sum(upper, axis=1, keepdims=True)
            two = two + jnp.sum(upper * value, axis=1, keepdims=True)
            backs[b, :, first : first + wide] = back
        moments = jnp.where(lane == 3 * i, one, jnp.where(lane == 3 * i + 1, two, moments))
        moments = jnp.where(lane == 3 * i + 2, loss, moments)
    high, low = split_sum(moments)
    turned = jnp.concatenate([high.astype(F32)[:, :32], low.astype(F32)[:, :32]], axis=1)
    zeros = jnp.zeros((ROWS, 32), F32)
    for half in range(2):
        mine[half] = backs[2 * half + c]
        mine[half, :, SPARE : SPARE + 64] = moments
        mine[half, :, BLOCK - 32 : BLOCK] = zeros
        other[half] = backs[2 * half + 1 - c].astype(BF16)
        other[half, :, SPARE : SPARE + 64] = turned.astype(BF16)
        other[half, :, BLOCK - 32 : BLOCK] = zeros.astype(BF16)


def grads_kernel(
    pos, n0, n1, n2, n3, e0, e1, e2, e3, keep, m1, m2, m3, total
):
    x = pos[X]
    for i in range(3):
        wide, first = QUARTERS[i], LINES[i]
        lines = jnp.concatenate([n[first : first + wide, :] for n in (n0, n1, n2, n3)], axis=1)
        errors = jnp.concatenate([e[i] for e in (e0, e1, e2, e3)], axis=0)
        total[first : first + wide, :] = dot(lines, errors)

    def piece(index):
        return (
            total[pl.ds(pl.multiple_of(index * 64, 8), 64), :],
            total[pl.ds(pl.multiple_of(256 + index * 48, 8), 48), :],
            total[pl.ds(pl.multiple_of(448 + index * 24, 8), 24), :],
        )

    keep[0:64, :], keep[64:112, :], keep[112:136, :] = piece(x)
    for step, out in ((1, m1), (2, m2), (3, m3)):
        large, base, small = piece(lax.rem(x + step, 4))
        out[0:64, :] = large.astype(BF16)
        out[64:112, :] = base.astype(BF16)
        out[112:144, :] = jnp.concatenate([small, jnp.zeros((8, 1024), F32)], axis=0).astype(BF16)


def back_kernel(pos, mine, got, keep, send, both):
    zh = pos[ZH]
    for half in range(2):
        both[half] = mine[half] + got[half].astype(F32)
    keep[...] = both[zh]
    send[...] = both[1 - zh].astype(BF16)
    value = both[0, :, SPARE : SPARE + 64]
    moments = value[:, 0:32] + value[:, 32:64]
    high, low = split_sum(moments)
    keep[:, SPARE : SPARE + 64] = jnp.concatenate([moments, jnp.zeros((ROWS, 32), F32)], axis=1)
    send[:, SPARE : SPARE + 64] = jnp.concatenate(
        [high.astype(F32), low.astype(F32)], axis=1
    ).astype(BF16)


def pieces_kernel(pos, keep, got, xhat, pieces):
    t = 2 * pos[ZH] + pos[C]
    back = keep[...] + got[...].astype(F32)
    moments = back[:, SPARE : SPARE + 32] + back[:, SPARE + 32 : SPARE + 64]
    terms = jnp.sum(back * xhat[t], axis=0, keepdims=True)
    pieces[...] = jnp.zeros_like(pieces)
    for j in range(5):
        pieces[j : j + 1, :] = terms[:, 128 * j : 128 * j + 128]
    pieces[5:6, 0:32] = jnp.sum(moments, axis=0, keepdims=True)


def rows_kernel(
    pos, keep, got, xhat, scales, place_t, gain_s, gain_b, gain_l, piece, piece_z, slots, gains
):
    t = 2 * pos[ZH] + pos[C]
    back = keep[...] + got[...].astype(F32)
    moments = back[:, SPARE : SPARE + 32] + back[:, SPARE + 32 : SPARE + 64]
    value = xhat[t]
    for i, gain in enumerate((gain_s, gain_b, gain_l)):
        wide = QUARTERS[i]
        for b in range(4):
            gains[b : b + 1, OFFSETS[i] : OFFSETS[i] + wide] = gain[:, b * wide : b * wide + wide]
    gain_row = gains[pl.ds(t, 1), :]
    pair = piece[...] + piece_z[...]
    high, low = split_sum(pair[5:6, 0:32])
    tail = jnp.concatenate(
        [pair[4:5], high.astype(F32), low.astype(F32), jnp.zeros((1, 64), F32)], axis=1
    )
    even = jnp.concatenate([jnp.concatenate([pair[0:1], pair[1:2]], axis=1), tail], axis=0)
    odd = jnp.concatenate([pair[2:3], pair[3:4]], axis=1)
    odd = jnp.concatenate([odd, jnp.zeros((1, 256), F32)], axis=0)
    spare = jnp.where(lax.rem(pos[ZL], 2) == 0, even, odd)
    spare = jnp.concatenate([spare, jnp.zeros((6, 256), F32)], axis=0)
    at = lax.broadcasted_iota(jnp.int32, (SHARDS * SLOT, 8), 0)
    kind = lax.broadcasted_iota(jnp.int32, (SHARDS * SLOT, 8), 1)
    ride = (lax.rem(at, SLOT) == CAP + kind).astype(F32).astype(BF16)
    slot = lax.broadcasted_iota(jnp.int32, (SHARDS * SLOT, ROWS), 0)
    total = dot(ride, spare.astype(BF16))
    for i in range(3):
        first, wide = OFFSETS[i], QUARTERS[i]
        hat = value[:, first : first + wide]
        upper = back[:, first : first + wide] * gain_row[:, first : first + wide]
        one = moments[:, 3 * i : 3 * i + 1] / WIDTHS[i]
        two = moments[:, 3 * i + 1 : 3 * i + 2] / WIDTHS[i]
        rows = scales[:, 128 * i : 128 * i + 1] * (upper - one - hat * two)
        if wide < 256:
            rows = jnp.concatenate([rows, jnp.zeros((ROWS, 256 - wide), F32)], axis=1)
        select = (slot == place_t[i : i + 1, :]).astype(F32).astype(BF16)
        total = total + dot(select, rows.astype(BF16))
    slots[...] = total.astype(BF16)


def third_kernel(pos, kept, p1, p2, p3, keep, m1, m2, m3, parts):
    zl = pos[ZL]
    total = kept[...] + sum(p[...].astype(F32)[0:136] for p in (p1, p2, p3))
    for i in range(4):
        parts[i, 0:16, :] = total[16 * i : 16 * i + 16]
        parts[i, 16:28, :] = total[64 + 12 * i : 64 + 12 * i + 12]
        parts[i, 28:34, :] = total[112 + 6 * i : 112 + 6 * i + 6]
        parts[i, 34:48, :] = jnp.zeros((14, 1024), F32)
    keep[...] = parts[zl]
    for step, out in ((1, m1), (2, m2), (3, m3)):
        out[...] = parts[lax.rem(zl + step, 4)].astype(BF16)


def last_kernel(pos, keep, m1, m2, m3, small, base, large):
    total = keep[...] + sum(p[...].astype(F32) for p in (m1, m2, m3))
    total = total / ROOT
    large[...] = total[0:16]
    base[...] = total[16:28]
    small[...] = total[28:34]


def sums_kernel(pos, got, gain_s, gain_b, gain_l, losses):
    slot = lax.broadcasted_iota(jnp.int32, (8, SHARDS * SLOT), 1)
    row = lax.broadcasted_iota(jnp.int32, (8, SHARDS * SLOT), 0)
    kind = 2 * lax.rem(lax.div(slot, SLOT), 2) + lax.rem(slot, SLOT) - CAP
    select = (lax.rem(slot, SLOT) >= CAP) & (kind == row)
    total = dot(select.astype(F32).astype(BF16), got[...])
    gain_l[...] = total[0:1] / ROOT
    gain_s[...] = total[1:2, 0:96] / ROOT
    gain_b[...] = total[2:3, 0:192] / ROOT
    loss = (total[1:2, 128:160] + total[1:2, 160:192]) / (2.0 * D * TOKENS)
    lane = lax.broadcasted_iota(jnp.int32, (1, 3), 1)
    losses[...] = jnp.where(
        lane == 0, loss[:, 2:3], jnp.where(lane == 1, loss[:, 5:6], loss[:, 8:9])
    )


def per_device(
    attn_out,
    out_proj,
    residual,
    teacher_gain,
    student_feats,
    head_small,
    head_base,
    head_large,
    gain_small,
    gain_base,
    gain_large,
    row_shard,
):
    pos = jnp.stack([lax.axis_index(a).astype(jnp.int32) for a in ("y", "x", "zl", "zh", "c")])
    tensor = 2 * pos[ZH] + pos[C]
    heads = (head_small, head_base, head_large)
    gains = (gain_small[None, :], gain_base[None, :], gain_large[None, :])

    own = out_proj.T
    early = [own] + [shifted(own, "zl", s) for s in (1, 2, 3)]
    weights = jnp.concatenate(early, axis=0)
    rows = [attn_out] + [shifted(attn_out, "y", s) for s in (1, 2, 3)]
    weights = [weights] + [shifted(weights, "x", s) for s in (1, 2, 3)]

    shard_t = jnp.pad(row_shard.T, ((0, 5), (0, 0)))
    shard_ids = jnp.arange(SHARDS, dtype=jnp.int32)
    named = (row_shard.T[:, :, None] == shard_ids[None, None, :]).astype(F32)
    own_counts = jnp.sum(named, axis=1).reshape(3 * SHARDS)
    feats = lax.dynamic_slice(student_feats, (0, tensor * 256), (SHARDS * CAP, 256))
    counts_row = jnp.pad(own_counts.astype(BF16), (0, 64))
    ride = jnp.broadcast_to(counts_row[None, None, :], (SHARDS, 2, 256))
    sent = jnp.concatenate([feats.reshape(SHARDS, CAP, 256), ride], axis=1)
    got = lax.all_to_all(sent, ("y", "x", "zl"), 0, 0, tiled=True).reshape(SHARDS * SLOT, 256)
    block, place_t, token_weights = call(
        place_kernel,
        [((ROWS, BLOCK), BF16), ((8, ROWS), jnp.int32), ((ROWS, 384), F32)],
        pos, row_shard, shard_t, got,
        flops=3 * 2 * 128 * 1024 * 256, moved=1 << 20,
    )
    block_c = swapped(block, "c")
    block_z = swapped(block, "zh")

    mine, other = call(
        teacher_kernel,
        [((2, ROWS, 1024), BF16)] * 2,
        pos, *rows, *weights,
        scratch=[((512, 1024), BF16), ((1024, 1024), BF16)],
        flops=2 * 512 * 1024 * 1024, moved=5 << 20, room=16,
    )
    first, second = call(
        pair_kernel, [((ROWS, 1024), BF16)] * 2, pos, mine, swapped(other, "c"), moved=2 << 20
    )
    parts = []
    for k, value in enumerate((first, second)):
        links = []
        for py in range(4):
            for pzh in range(2):
                for pc in range(2):
                    links.append(((py * 2 + pzh) * 2 + pc, (pc + 2 * ((pzh + k) % 2)) * 4 + py))
        parts.append(lax.ppermute(value, ("y", "zh", "c"), links))


    hidden, sums = call(
        hidden_kernel, [((ROWS, 1024), F32), ((8, ROWS), F32)], pos, *parts, residual, moved=1 << 20
    )
    block_z, hidden = lax.optimization_barrier((block_z, hidden))
    block_zc = swapped(block_z, "c")
    xhat, scales, outs, *lines = call(
        student_kernel,
        [
            ((4, ROWS, BLOCK), F32),
            ((ROWS, 384), F32),
            ((3, ROWS, 1024), F32),
        ]
        + [((544, ROWS), BF16)] * 4,
        pos, block, block_c, block_z, block_zc, *gains, *heads,
        scratch=[((4, ROWS, BLOCK), BF16), ((4, 544, ROWS), BF16)],
        flops=2 * 128 * 2176 * 1024, moved=9 << 20, room=20,
    )
    sums = sums + swapped(sums, "c")
    sums = sums + swapped(sums, "zh")

    lines = [lines[0]] + [shifted(lines[s], "y", s) for s in (1, 2, 3)]
    sums, lines = lax.optimization_barrier((sums, lines))
    errors, mine, other = call(
        error_kernel,
        [((3, ROWS, 1024), BF16), ((2, ROWS, BLOCK), F32), ((2, ROWS, BLOCK), BF16)],
        pos, hidden, sums, teacher_gain[None, :], outs, token_weights, xhat,
        *gains, *heads,
        scratch=[((4, ROWS, BLOCK), F32)],
        flops=4 * 128 * 2176 * 1024, moved=15 << 20, room=28,
    )
    errors = [errors] + [shifted(errors, "y", s) for s in (1, 2, 3)]

    got = swapped(other, "c")
    keep, send = call(
        back_kernel,
        [((ROWS, BLOCK), F32), ((ROWS, BLOCK), BF16)],
        pos, mine, got,
        scratch=[((2, ROWS, BLOCK), F32)], moved=2 << 20,
    )
    got = swapped(send, "zh")
    (pieces,) = call(pieces_kernel, [((8, 128), F32)], pos, keep, got, xhat, moved=1 << 20)
    pieces_z = lax.ppermute(pieces, "zl", [(0, 1), (1, 0), (2, 3), (3, 2)])
    (slots,) = call(
        rows_kernel,
        [((SHARDS * SLOT, 256), BF16)],
        pos, keep, got, xhat, scales, place_t, *gains, pieces, pieces_z,
        scratch=[((8, BLOCK), F32)],
        flops=3 * 2 * 128 * 1024 * 256, moved=2 << 20,
    )
    got = lax.all_to_all(slots.reshape(SHARDS, SLOT, 256), ("y", "x", "zl"), 0, 0, tiled=True)
    token_gradient = got[:, :CAP].reshape(SHARDS * CAP, 256)
    gain_s, gain_b, gain_l, losses = call(
        sums_kernel,
        [((1, n), F32) for n in (96, 192, 256, 3)],
        pos, got.reshape(SHARDS * SLOT, 256), moved=1 << 19,
    )

    keep, *sent = call(
        grads_kernel,
        [((136, 1024), F32)] + [((144, 1024), BF16)] * 3,
        pos, *lines, *errors,
        scratch=[((544, 1024), F32)], flops=2 * 512 * 544 * 1024, moved=5 << 20, room=16,
    )
    keep, *sent = call(
        third_kernel,
        [((48, 1024), F32)] + [((48, 1024), BF16)] * 3,
        pos, keep, *[shifted(sent[s - 1], "x", s) for s in (1, 2, 3)],
        scratch=[((4, 48, 1024), F32)], moved=2 << 20,
    )
    sent = [shifted(sent[s - 1], "zl", s) for s in (1, 2, 3)]
    sent, token_gradient, gain_s, gain_b, gain_l, losses = lax.optimization_barrier(
        (sent, token_gradient, gain_s, gain_b, gain_l, losses)
    )
    grad_small, grad_base, grad_large = call(
        last_kernel,
        [((6, 1024), F32), ((12, 1024), F32), ((16, 1024), F32)],
        pos, keep, *sent,
        moved=1 << 20,
    )
    return (
        grad_small,
        grad_base,
        grad_large,
        gain_s[0],
        gain_b[0],
        gain_l[0],
        token_gradient,
        losses[0],
    )


def solution(mesh):
    fine = Mesh(mesh.devices.reshape(4, 4, 4, 2, 2), ("y", "x", "zl", "zh", "c"))
    dp = ("y", "x", "zl")
    tp = ("zh", "c")
    return jax.shard_map(
        per_device,
        mesh=fine,
        in_specs=(
            P(dp, tp),
            P(tp, dp),
            P(dp, tp),
            P(tp),
            P(dp, None),
            P(None, tp),
            P(None, tp),
            P(None, tp),
            P(),
            P(),
            P(),
            P(dp, None),
        ),
        out_specs=(
            P(dp, tp),
            P(dp, tp),
            P(dp, tp),
            P(tp),
            P(tp),
            P(tp),
            P(dp, tp),
            P(),
        ),
        check_vma=False,
    )
```

```python
import functools
import math

import jax
import jax.numpy as jnp
from jax import lax
from jax.experimental import pallas as pl
from jax.experimental.pallas import tpu as pltpu
from jax.sharding import Mesh
from jax.sharding import PartitionSpec as P

D = 4096
TOKENS = 8192
ROWS = 128
SHARDS = 64
CAP = 14
SLOT = 16
GROUPS = (12, 20, 32)
WIDTHS = (384, 768, 1024)
QUARTERS = (96, 192, 256)
OFFSETS = (512, 256, 0)
BLOCK = 640
LINES = (448, 256, 0)
SPARE = 448
ROOT = math.sqrt(TOKENS)
F32 = jnp.float32
BF16 = jnp.bfloat16
SWAP = [(0, 1), (1, 0)]
MIB = 1024 * 1024


def call(body, outs, *args, scratch=(), flops=0, moved=0, room=8):
    specs = [pl.BlockSpec(memory_space=pltpu.SMEM)]
    specs += [pl.BlockSpec(memory_space=pltpu.VMEM)] * (len(args) - 1)
    return pl.pallas_call(
        body,
        out_shape=[jax.ShapeDtypeStruct(shape, dtype) for shape, dtype in outs],
        in_specs=specs,
        out_specs=[pl.BlockSpec(memory_space=pltpu.VMEM)] * len(outs),
        scratch_shapes=[pltpu.VMEM(shape, dtype) for shape, dtype in scratch],
        compiler_params=pltpu.CompilerParams(vmem_limit_bytes=room * MIB),
        cost_estimate=pl.CostEstimate(flops=flops, bytes_accessed=moved, transcendentals=0),
    )(*args)


def dot(a, b):
    return jnp.dot(a, b, preferred_element_type=F32)


def dot_t(a, b):
    return lax.dot_general(a, b, (((1,), (1,)), ((), ())), preferred_element_type=F32)


def shifted(value, axis, step):
    return lax.ppermute(value, axis, [(i, (i + step) % 4) for i in range(4)])


def swapped(value, axis):
    return lax.ppermute(value, axis, SWAP)


def split_sum(value):
    high = value.astype(BF16)
    return high, (value - high.astype(F32)).astype(BF16)


Y, X, ZL, ZH, C = range(5)


def teacher_kernel(pos, a0, a1, a2, a3, w0, w1, w2, w3, mine, other, rows, weights):
    y, x, zl, c = pos[Y], pos[X], pos[ZL], pos[C]
    for step, part in enumerate((a0, a1, a2, a3)):
        index = lax.rem(y + 4 - step, 4)
        place = 2 * lax.rem(index + c, 2) + lax.div(index, 2)
        rows[pl.ds(pl.multiple_of(place * ROWS, ROWS), ROWS), :] = part[...]
    for step, part in enumerate((w0, w1, w2, w3)):
        first = lax.rem(x + 4 - step, 4) * 256
        for turn in range(4):
            start = pl.multiple_of(first + lax.rem(zl + 4 - turn, 4) * 64, 64)
            weights[pl.ds(start, 64), :] = part[turn * 64 : turn * 64 + 64, :]
    product = dot_t(rows[...], weights[...]).astype(BF16)
    for half in range(2):
        mine[half] = product[half * ROWS : half * ROWS + ROWS]
        other[half] = product[(half + 2) * ROWS : (half + 3) * ROWS]


def pair_kernel(pos, mine, got, first, second):
    zh = pos[ZH]
    first[...] = (mine[zh].astype(F32) + got[zh].astype(F32)).astype(BF16)
    second[...] = (mine[1 - zh].astype(F32) + got[1 - zh].astype(F32)).astype(BF16)


def hidden_kernel(pos, first, second, residual, hidden, sums):
    value = residual[...].astype(F32) + (first[...].astype(F32) + second[...].astype(F32))
    hidden[...] = value
    lane = lax.broadcasted_iota(jnp.int32, (ROWS, 128), 1)
    total = jnp.sum(value, axis=1, keepdims=True)
    square = jnp.sum(value * value, axis=1, keepdims=True)
    both = jnp.where(lane == 0, total, jnp.where(lane == 1, square, 0.0))
    sums[...] = jnp.transpose(both)[0:8]


def place_kernel(pos, shard, shard_t, got, block, place_t, weights):
    token = lax.broadcasted_iota(jnp.int32, (ROWS, ROWS), 0)
    token_t = lax.broadcasted_iota(jnp.int32, (ROWS, ROWS), 1)
    slot = lax.broadcasted_iota(jnp.int32, (ROWS, SHARDS * SLOT), 1)
    spare = lax.broadcasted_iota(jnp.int32, (8, SHARDS * SLOT), 1)
    lane = lax.broadcasted_iota(jnp.int32, (ROWS, 256), 1)
    counts = dot((lax.rem(spare, SLOT) == CAP).astype(F32).astype(BF16), got[...])[0:1]
    block[...] = jnp.zeros_like(block)
    place_t[...] = jnp.zeros_like(place_t)
    for i in range(3):
        column = shard[:, i : i + 1]
        row = shard_t[i : i + 1, :]
        same = column == row
        rank = jnp.sum(jnp.where(same & (token_t < token), 1, 0), axis=1, keepdims=True)
        rank_t = jnp.sum(jnp.where(same & (token < token_t), 1, 0), axis=0, keepdims=True)
        place_t[i : i + 1, :] = row * SLOT + rank_t
        select = (slot == column * SLOT + rank).astype(F32).astype(BF16)
        value = dot(select, got[...]).astype(BF16)
        block[:, OFFSETS[i] : OFFSETS[i] + QUARTERS[i]] = value[:, : QUARTERS[i]]
        owned = jnp.sum(jnp.where(lane == column + 64 * i, counts, 0.0), axis=1, keepdims=True)
        weights[:, 128 * i : 128 * i + 128] = jnp.broadcast_to(
            TOKENS / (GROUPS[i] * owned), (ROWS, 128)
        )


def student_kernel(
    pos, own, own_c, own_z, own_zc, gain_s, gain_b, gain_l, head_s, head_b, head_l,
    xhat, scales, outs, n0, n1, n2, n3, blocks, lines,
):
    y, zh, c = pos[Y], pos[ZH], pos[C]
    blocks[2 * zh + c] = own[...]
    blocks[2 * zh + 1 - c] = own_c[...]
    blocks[2 * (1 - zh) + c] = own_z[...]
    blocks[2 * (1 - zh) + 1 - c] = own_zc[...]
    xhat[...] = jnp.zeros_like(xhat)
    for i, (gain, head) in enumerate(((gain_s, head_s), (gain_b, head_b), (gain_l, head_l))):
        wide, first, first_line = QUARTERS[i], OFFSETS[i], LINES[i]
        parts = [blocks[b, :, first : first + wide].astype(F32) for b in range(4)]
        total = sum(jnp.sum(p, axis=1, keepdims=True) for p in parts)
        square = sum(jnp.sum(p * p, axis=1, keepdims=True) for p in parts)
        center = total / WIDTHS[i]
        scale = lax.rsqrt(square / WIDTHS[i] - center * center + 1e-06)
        scales[:, 128 * i : 128 * i + 128] = jnp.broadcast_to(scale, (ROWS, 128))
        out = jnp.zeros((ROWS, 1024), F32)
        for b in range(4):
            value = (parts[b] - center) * scale
            xhat[b, :, first : first + wide] = value
            normed = value * gain[:, b * wide : b * wide + wide]
            out = out + dot(normed.astype(BF16), head[b * wide : b * wide + wide, :])
            lines[b, first_line : first_line + wide, :] = jnp.transpose(normed).astype(BF16)
        outs[i] = out
    for step, out in enumerate((n0, n1, n2, n3)):
        out[...] = lines[lax.rem(y + step, 4)]


def error_kernel(
    pos, hidden, sums, teacher_gain, outs, weights, xhat,
    gain_s, gain_b, gain_l, head_s, head_b, head_l,
    errors, mine, other, backs,
):
    c = pos[C]
    stats = jnp.transpose(jnp.concatenate([sums[...], jnp.zeros((120, 128), F32)], axis=0))
    center = stats[:, 0:1] / D
    spread = stats[:, 1:2] / D - center * center
    target = (hidden[...] - center) * lax.rsqrt(spread + 1e-06) * teacher_gain[...]
    target = target.astype(BF16).astype(F32)
    lane = lax.broadcasted_iota(jnp.int32, (ROWS, 64), 1)
    moments = jnp.zeros((ROWS, 64), F32)
    for i, (gain, head) in enumerate(((gain_s, head_s), (gain_b, head_b), (gain_l, head_l))):
        wide, first = QUARTERS[i], OFFSETS[i]
        weight = weights[:, 128 * i : 128 * i + 1]
        diff = outs[i] - target
        error = (weight * diff).astype(BF16)
        errors[i] = error
        loss = weight * jnp.sum(diff * diff, axis=1, keepdims=True)
        one = jnp.zeros((ROWS, 1), F32)
        two = jnp.zeros((ROWS, 1), F32)
        for b in range(4):
            back = dot_t(error, head[b * wide : b * wide + wide, :])
            value = xhat[b, :, first : first + wide]
            upper = back * gain[:, b * wide : b * wide + wide]
            one = one + jnp.sum(upper, axis=1, keepdims=True)
            two = two + jnp.sum(upper * value, axis=1, keepdims=True)
            backs[b, :, first : first + wide] = back
        moments = jnp.where(lane == 3 * i, one, jnp.where(lane == 3 * i + 1, two, moments))
        moments = jnp.where(lane == 3 * i + 2, loss, moments)
    high, low = split_sum(moments)
    turned = jnp.concatenate([high.astype(F32)[:, :32], low.astype(F32)[:, :32]], axis=1)
    zeros = jnp.zeros((ROWS, 32), F32)
    for half in range(2):
        mine[half] = backs[2 * half + c]
        mine[half, :, SPARE : SPARE + 64] = moments
        mine[half, :, BLOCK - 32 : BLOCK] = zeros
        other[half] = backs[2 * half + 1 - c].astype(BF16)
        other[half, :, SPARE : SPARE + 64] = turned.astype(BF16)
        other[half, :, BLOCK - 32 : BLOCK] = zeros.astype(BF16)


def grads_kernel(
    pos, n0, n1, n2, n3, e0, e1, e2, e3, keep, m1, m2, m3, total
):
    x = pos[X]
    for i in range(3):
        wide, first = QUARTERS[i], LINES[i]
        lines = jnp.concatenate([n[first : first + wide, :] for n in (n0, n1, n2, n3)], axis=1)
        errors = jnp.concatenate([e[i] for e in (e0, e1, e2, e3)], axis=0)
        total[first : first + wide, :] = dot(lines, errors)

    def piece(index):
        return (
            total[pl.ds(pl.multiple_of(index * 64, 8), 64), :],
            total[pl.ds(pl.multiple_of(256 + index * 48, 8), 48), :],
            total[pl.ds(pl.multiple_of(448 + index * 24, 8), 24), :],
        )

    keep[0:64, :], keep[64:112, :], keep[112:136, :] = piece(x)
    for step, out in ((1, m1), (2, m2), (3, m3)):
        large, base, small = piece(lax.rem(x + step, 4))
        out[0:64, :] = large.astype(BF16)
        out[64:112, :] = base.astype(BF16)
        out[112:144, :] = jnp.concatenate([small, jnp.zeros((8, 1024), F32)], axis=0).astype(BF16)


def back_kernel(pos, mine, got, keep, send, both):
    zh = pos[ZH]
    for half in range(2):
        both[half] = mine[half] + got[half].astype(F32)
    keep[...] = both[zh]
    send[...] = both[1 - zh].astype(BF16)
    value = both[0, :, SPARE : SPARE + 64]
    moments = value[:, 0:32] + value[:, 32:64]
    high, low = split_sum(moments)
    keep[:, SPARE : SPARE + 64] = jnp.concatenate([moments, jnp.zeros((ROWS, 32), F32)], axis=1)
    send[:, SPARE : SPARE + 64] = jnp.concatenate(
        [high.astype(F32), low.astype(F32)], axis=1
    ).astype(BF16)


def pieces_kernel(pos, keep, got, xhat, pieces):
    t = 2 * pos[ZH] + pos[C]
    back = keep[...] + got[...].astype(F32)
    moments = back[:, SPARE : SPARE + 32] + back[:, SPARE + 32 : SPARE + 64]
    terms = jnp.sum(back * xhat[t], axis=0, keepdims=True)
    pieces[...] = jnp.zeros_like(pieces)
    for j in range(5):
        pieces[j : j + 1, :] = terms[:, 128 * j : 128 * j + 128]
    pieces[5:6, 0:32] = jnp.sum(moments, axis=0, keepdims=True)


def rows_kernel(
    pos, keep, got, xhat, scales, place_t, gain_s, gain_b, gain_l, piece, piece_z, slots, gains
):
    t = 2 * pos[ZH] + pos[C]
    back = keep[...] + got[...].astype(F32)
    moments = back[:, SPARE : SPARE + 32] + back[:, SPARE + 32 : SPARE + 64]
    value = xhat[t]
    for i, gain in enumerate((gain_s, gain_b, gain_l)):
        wide = QUARTERS[i]
        for b in range(4):
            gains[b : b + 1, OFFSETS[i] : OFFSETS[i] + wide] = gain[:, b * wide : b * wide + wide]
    gain_row = gains[pl.ds(t, 1), :]
    pair = piece[...] + piece_z[...]
    high, low = split_sum(pair[5:6, 0:32])
    tail = jnp.concatenate(
        [pair[4:5], high.astype(F32), low.astype(F32), jnp.zeros((1, 64), F32)], axis=1
    )
    even = jnp.concatenate([jnp.concatenate([pair[0:1], pair[1:2]], axis=1), tail], axis=0)
    odd = jnp.concatenate([pair[2:3], pair[3:4]], axis=1)
    odd = jnp.concatenate([odd, jnp.zeros((1, 256), F32)], axis=0)
    spare = jnp.where(lax.rem(pos[ZL], 2) == 0, even, odd)
    spare = jnp.concatenate([spare, jnp.zeros((6, 256), F32)], axis=0)
    at = lax.broadcasted_iota(jnp.int32, (SHARDS * SLOT, 8), 0)
    kind = lax.broadcasted_iota(jnp.int32, (SHARDS * SLOT, 8), 1)
    ride = (lax.rem(at, SLOT) == CAP + kind).astype(F32).astype(BF16)
    slot = lax.broadcasted_iota(jnp.int32, (SHARDS * SLOT, ROWS), 0)
    total = dot(ride, spare.astype(BF16))
    for i in range(3):
        first, wide = OFFSETS[i], QUARTERS[i]
        hat = value[:, first : first + wide]
        upper = back[:, first : first + wide] * gain_row[:, first : first + wide]
        one = moments[:, 3 * i : 3 * i + 1] / WIDTHS[i]
        two = moments[:, 3 * i + 1 : 3 * i + 2] / WIDTHS[i]
        rows = scales[:, 128 * i : 128 * i + 1] * (upper - one - hat * two)
        if wide < 256:
            rows = jnp.concatenate([rows, jnp.zeros((ROWS, 256 - wide), F32)], axis=1)
        select = (slot == place_t[i : i + 1, :]).astype(F32).astype(BF16)
        total = total + dot(select, rows.astype(BF16))
    slots[...] = total.astype(BF16)


def third_kernel(pos, kept, p1, p2, p3, keep, m1, m2, m3, parts):
    zl = pos[ZL]
    total = kept[...] + sum(p[...].astype(F32)[0:136] for p in (p1, p2, p3))
    for i in range(4):
        parts[i, 0:16, :] = total[16 * i : 16 * i + 16]
        parts[i, 16:28, :] = total[64 + 12 * i : 64 + 12 * i + 12]
        parts[i, 28:34, :] = total[112 + 6 * i : 112 + 6 * i + 6]
        parts[i, 34:48, :] = jnp.zeros((14, 1024), F32)
    keep[...] = parts[zl]
    for step, out in ((1, m1), (2, m2), (3, m3)):
        out[...] = parts[lax.rem(zl + step, 4)].astype(BF16)


def last_kernel(pos, keep, m1, m2, m3, small, base, large):
    total = keep[...] + sum(p[...].astype(F32) for p in (m1, m2, m3))
    total = total / ROOT
    large[...] = total[0:16]
    base[...] = total[16:28]
    small[...] = total[28:34]


def sums_kernel(pos, got, gain_s, gain_b, gain_l, losses):
    slot = lax.broadcasted_iota(jnp.int32, (8, SHARDS * SLOT), 1)
    row = lax.broadcasted_iota(jnp.int32, (8, SHARDS * SLOT), 0)
    kind = 2 * lax.rem(lax.div(slot, SLOT), 2) + lax.rem(slot, SLOT) - CAP
    select = (lax.rem(slot, SLOT) >= CAP) & (kind == row)
    total = dot(select.astype(F32).astype(BF16), got[...])
    gain_l[...] = total[0:1] / ROOT
    gain_s[...] = total[1:2, 0:96] / ROOT
    gain_b[...] = total[2:3, 0:192] / ROOT
    loss = (total[1:2, 128:160] + total[1:2, 160:192]) / (2.0 * D * TOKENS)
    lane = lax.broadcasted_iota(jnp.int32, (1, 3), 1)
    losses[...] = jnp.where(
        lane == 0, loss[:, 2:3], jnp.where(lane == 1, loss[:, 5:6], loss[:, 8:9])
    )


def per_device(
    attn_out,
    out_proj,
    residual,
    teacher_gain,
    student_feats,
    head_small,
    head_base,
    head_large,
    gain_small,
    gain_base,
    gain_large,
    row_shard,
):
    pos = jnp.stack([lax.axis_index(a).astype(jnp.int32) for a in ("y", "x", "zl", "zh", "c")])
    tensor = 2 * pos[ZH] + pos[C]
    heads = (head_small, head_base, head_large)
    gains = (gain_small[None, :], gain_base[None, :], gain_large[None, :])

    own = out_proj.T
    early = [own] + [shifted(own, "zl", s) for s in (1, 2, 3)]
    weights = jnp.concatenate(early, axis=0)
    rows = [attn_out] + [shifted(attn_out, "y", s) for s in (1, 2, 3)]
    weights = [weights] + [shifted(weights, "x", s) for s in (1, 2, 3)]

    shard_t = jnp.pad(row_shard.T, ((0, 5), (0, 0)))
    shard_ids = jnp.arange(SHARDS, dtype=jnp.int32)
    named = (row_shard.T[:, :, None] == shard_ids[None, None, :]).astype(F32)
    own_counts = jnp.sum(named, axis=1).reshape(3 * SHARDS)
    feats = lax.dynamic_slice(student_feats, (0, tensor * 256), (SHARDS * CAP, 256))
    counts_row = jnp.pad(own_counts.astype(BF16), (0, 64))
    ride = jnp.broadcast_to(counts_row[None, None, :], (SHARDS, 2, 256))
    sent = jnp.concatenate([feats.reshape(SHARDS, CAP, 256), ride], axis=1)
    got = lax.all_to_all(sent, ("y", "x", "zl"), 0, 0, tiled=True).reshape(SHARDS * SLOT, 256)
    block, place_t, token_weights = call(
        place_kernel,
        [((ROWS, BLOCK), BF16), ((8, ROWS), jnp.int32), ((ROWS, 384), F32)],
        pos, row_shard, shard_t, got,
        flops=3 * 2 * 128 * 1024 * 256, moved=1 << 20,
    )
    block_c = swapped(block, "c")
    block_z = swapped(block, "zh")

    mine, other = call(
        teacher_kernel,
        [((2, ROWS, 1024), BF16)] * 2,
        pos, *rows, *weights,
        scratch=[((512, 1024), BF16), ((1024, 1024), BF16)],
        flops=2 * 512 * 1024 * 1024, moved=5 << 20, room=16,
    )
    first, second = call(
        pair_kernel, [((ROWS, 1024), BF16)] * 2, pos, mine, swapped(other, "c"), moved=2 << 20
    )
    parts = []
    for k, value in enumerate((first, second)):
        links = []
        for py in range(4):
            for pzh in range(2):
                for pc in range(2):
                    links.append(((py * 2 + pzh) * 2 + pc, (pc + 2 * ((pzh + k) % 2)) * 4 + py))
        parts.append(lax.ppermute(value, ("y", "zh", "c"), links))


    hidden, sums = call(
        hidden_kernel, [((ROWS, 1024), F32), ((8, ROWS), F32)], pos, *parts, residual, moved=1 << 20
    )
    block_z, hidden = lax.optimization_barrier((block_z, hidden))
    block_zc = swapped(block_z, "c")
    xhat, scales, outs, *lines = call(
        student_kernel,
        [
            ((4, ROWS, BLOCK), F32),
            ((ROWS, 384), F32),
            ((3, ROWS, 1024), F32),
        ]
        + [((544, ROWS), BF16)] * 4,
        pos, block, block_c, block_z, block_zc, *gains, *heads,
        scratch=[((4, ROWS, BLOCK), BF16), ((4, 544, ROWS), BF16)],
        flops=2 * 128 * 2176 * 1024, moved=9 << 20, room=20,
    )
    sums = sums + swapped(sums, "c")
    sums = sums + swapped(sums, "zh")

    lines = [lines[0]] + [shifted(lines[s], "y", s) for s in (1, 2, 3)]
    sums, lines = lax.optimization_barrier((sums, lines))
    errors, mine, other = call(
        error_kernel,
        [((3, ROWS, 1024), BF16), ((2, ROWS, BLOCK), F32), ((2, ROWS, BLOCK), BF16)],
        pos, hidden, sums, teacher_gain[None, :], outs, token_weights, xhat,
        *gains, *heads,
        scratch=[((4, ROWS, BLOCK), F32)],
        flops=4 * 128 * 2176 * 1024, moved=15 << 20, room=28,
    )
    errors = [errors] + [shifted(errors, "y", s) for s in (1, 2, 3)]

    got = swapped(other, "c")
    keep, send = call(
        back_kernel,
        [((ROWS, BLOCK), F32), ((ROWS, BLOCK), BF16)],
        pos, mine, got,
        scratch=[((2, ROWS, BLOCK), F32)], moved=2 << 20,
    )
    got = swapped(send, "zh")
    (pieces,) = call(pieces_kernel, [((8, 128), F32)], pos, keep, got, xhat, moved=1 << 20)
    pieces_z = lax.ppermute(pieces, "zl", [(0, 1), (1, 0), (2, 3), (3, 2)])
    (slots,) = call(
        rows_kernel,
        [((SHARDS * SLOT, 256), BF16)],
        pos, keep, got, xhat, scales, place_t, *gains, pieces, pieces_z,
        scratch=[((8, BLOCK), F32)],
        flops=3 * 2 * 128 * 1024 * 256, moved=2 << 20,
    )
    slots, errors[1], errors[2], errors[3] = lax.optimization_barrier((slots, *errors[1:]))
    got = lax.all_to_all(slots.reshape(SHARDS, SLOT, 256), ("y", "x", "zl"), 0, 0, tiled=True)
    token_gradient = got[:, :CAP].reshape(SHARDS * CAP, 256)
    gain_s, gain_b, gain_l, losses = call(
        sums_kernel,
        [((1, n), F32) for n in (96, 192, 256, 3)],
        pos, got.reshape(SHARDS * SLOT, 256), moved=1 << 19,
    )

    keep, *sent = call(
        grads_kernel,
        [((136, 1024), F32)] + [((144, 1024), BF16)] * 3,
        pos, *lines, *errors,
        scratch=[((544, 1024), F32)], flops=2 * 512 * 544 * 1024, moved=5 << 20, room=16,
    )
    keep, *sent = call(
        third_kernel,
        [((48, 1024), F32)] + [((48, 1024), BF16)] * 3,
        pos, keep, *[shifted(sent[s - 1], "x", s) for s in (1, 2, 3)],
        scratch=[((4, 48, 1024), F32)], moved=2 << 20,
    )
    sent = [shifted(sent[s - 1], "zl", s) for s in (1, 2, 3)]
    sent, token_gradient, gain_s, gain_b, gain_l, losses = lax.optimization_barrier(
        (sent, token_gradient, gain_s, gain_b, gain_l, losses)
    )
    grad_small, grad_base, grad_large = call(
        last_kernel,
        [((6, 1024), F32), ((12, 1024), F32), ((16, 1024), F32)],
        pos, keep, *sent,
        moved=1 << 20,
    )
    return (
        grad_small,
        grad_base,
        grad_large,
        gain_s[0],
        gain_b[0],
        gain_l[0],
        token_gradient,
        losses[0],
    )


def solution(mesh):
    fine = Mesh(mesh.devices.reshape(4, 4, 4, 2, 2), ("y", "x", "zl", "zh", "c"))
    dp = ("y", "x", "zl")
    tp = ("zh", "c")
    return jax.shard_map(
        per_device,
        mesh=fine,
        in_specs=(
            P(dp, tp),
            P(tp, dp),
            P(dp, tp),
            P(tp),
            P(dp, None),
            P(None, tp),
            P(None, tp),
            P(None, tp),
            P(),
            P(),
            P(),
            P(dp, None),
        ),
        out_specs=(
            P(dp, tp),
            P(dp, tp),
            P(dp, tp),
            P(tp),
            P(tp),
            P(tp),
            P(dp, tp),
            P(),
        ),
        check_vma=False,
    )
```

```python
import functools
import math

import jax
import jax.numpy as jnp
from jax import lax
from jax.experimental import pallas as pl
from jax.experimental.pallas import tpu as pltpu
from jax.sharding import Mesh
from jax.sharding import PartitionSpec as P

D = 4096
TOKENS = 8192
ROWS = 128
SHARDS = 64
CAP = 14
SLOT = 16
GROUPS = (12, 20, 32)
WIDTHS = (384, 768, 1024)
QUARTERS = (96, 192, 256)
OFFSETS = (512, 256, 0)
BLOCK = 640
LINES = (448, 256, 0)
SPARE = 448
ROOT = math.sqrt(TOKENS)
F32 = jnp.float32
BF16 = jnp.bfloat16
SWAP = [(0, 1), (1, 0)]
MIB = 1024 * 1024


def call(body, outs, *args, scratch=(), flops=0, moved=0, room=8):
    specs = [pl.BlockSpec(memory_space=pltpu.SMEM)]
    specs += [pl.BlockSpec(memory_space=pltpu.VMEM)] * (len(args) - 1)
    return pl.pallas_call(
        body,
        out_shape=[jax.ShapeDtypeStruct(shape, dtype) for shape, dtype in outs],
        in_specs=specs,
        out_specs=[pl.BlockSpec(memory_space=pltpu.VMEM)] * len(outs),
        scratch_shapes=[pltpu.VMEM(shape, dtype) for shape, dtype in scratch],
        compiler_params=pltpu.CompilerParams(vmem_limit_bytes=room * MIB),
        cost_estimate=pl.CostEstimate(flops=flops, bytes_accessed=moved, transcendentals=0),
    )(*args)


def dot(a, b):
    return jnp.dot(a, b, preferred_element_type=F32)


def dot_t(a, b):
    return lax.dot_general(a, b, (((1,), (1,)), ((), ())), preferred_element_type=F32)


def shifted(value, axis, step):
    return lax.ppermute(value, axis, [(i, (i + step) % 4) for i in range(4)])


def swapped(value, axis):
    return lax.ppermute(value, axis, SWAP)


def split_sum(value):
    high = value.astype(BF16)
    return high, (value - high.astype(F32)).astype(BF16)


Y, X, ZL, ZH, C = range(5)


def teacher_kernel(pos, a0, a1, a2, a3, w0, w1, w2, w3, mine, other, rows, weights):
    y, x, zl, c = pos[Y], pos[X], pos[ZL], pos[C]
    for step, part in enumerate((a0, a1, a2, a3)):
        index = lax.rem(y + 4 - step, 4)
        place = 2 * lax.rem(index + c, 2) + lax.div(index, 2)
        rows[pl.ds(pl.multiple_of(place * ROWS, ROWS), ROWS), :] = part[...]
    for step, part in enumerate((w0, w1, w2, w3)):
        first = lax.rem(x + 4 - step, 4) * 256
        for turn in range(4):
            start = pl.multiple_of(first + lax.rem(zl + 4 - turn, 4) * 64, 64)
            weights[pl.ds(start, 64), :] = part[turn * 64 : turn * 64 + 64, :]
    product = dot_t(rows[...], weights[...]).astype(BF16)
    for half in range(2):
        mine[half] = product[half * ROWS : half * ROWS + ROWS]
        other[half] = product[(half + 2) * ROWS : (half + 3) * ROWS]


def pair_kernel(pos, mine, got, first, second):
    zh = pos[ZH]
    first[...] = (mine[zh].astype(F32) + got[zh].astype(F32)).astype(BF16)
    second[...] = (mine[1 - zh].astype(F32) + got[1 - zh].astype(F32)).astype(BF16)


def hidden_kernel(pos, first, second, residual, hidden, sums):
    value = residual[...].astype(F32) + (first[...].astype(F32) + second[...].astype(F32))
    hidden[...] = value
    lane = lax.broadcasted_iota(jnp.int32, (ROWS, 128), 1)
    total = jnp.sum(value, axis=1, keepdims=True)
    square = jnp.sum(value * value, axis=1, keepdims=True)
    both = jnp.where(lane == 0, total, jnp.where(lane == 1, square, 0.0))
    sums[...] = jnp.transpose(both)[0:8]


def place_kernel(pos, shard, shard_t, got, block, place_t, weights):
    token = lax.broadcasted_iota(jnp.int32, (ROWS, ROWS), 0)
    token_t = lax.broadcasted_iota(jnp.int32, (ROWS, ROWS), 1)
    slot = lax.broadcasted_iota(jnp.int32, (ROWS, SHARDS * SLOT), 1)
    spare = lax.broadcasted_iota(jnp.int32, (8, SHARDS * SLOT), 1)
    lane = lax.broadcasted_iota(jnp.int32, (ROWS, 256), 1)
    counts = dot((lax.rem(spare, SLOT) == CAP).astype(F32).astype(BF16), got[...])[0:1]
    block[...] = jnp.zeros_like(block)
    place_t[...] = jnp.zeros_like(place_t)
    for i in range(3):
        column = shard[:, i : i + 1]
        row = shard_t[i : i + 1, :]
        same = column == row
        rank = jnp.sum(jnp.where(same & (token_t < token), 1, 0), axis=1, keepdims=True)
        rank_t = jnp.sum(jnp.where(same & (token < token_t), 1, 0), axis=0, keepdims=True)
        place_t[i : i + 1, :] = row * SLOT + rank_t
        select = (slot == column * SLOT + rank).astype(F32).astype(BF16)
        value = dot(select, got[...]).astype(BF16)
        block[:, OFFSETS[i] : OFFSETS[i] + QUARTERS[i]] = value[:, : QUARTERS[i]]
        owned = jnp.sum(jnp.where(lane == column + 64 * i, counts, 0.0), axis=1, keepdims=True)
        weights[:, 128 * i : 128 * i + 128] = jnp.broadcast_to(
            TOKENS / (GROUPS[i] * owned), (ROWS, 128)
        )


def student_kernel(
    pos, own, own_c, own_z, own_zc, gain_s, gain_b, gain_l, head_s, head_b, head_l,
    xhat, scales, outs, n0, n1, n2, n3, blocks, lines,
):
    y, zh, c = pos[Y], pos[ZH], pos[C]
    blocks[2 * zh + c] = own[...]
    blocks[2 * zh + 1 - c] = own_c[...]
    blocks[2 * (1 - zh) + c] = own_z[...]
    blocks[2 * (1 - zh) + 1 - c] = own_zc[...]
    xhat[...] = jnp.zeros_like(xhat)
    for i, (gain, head) in enumerate(((gain_s, head_s), (gain_b, head_b), (gain_l, head_l))):
        wide, first, first_line = QUARTERS[i], OFFSETS[i], LINES[i]
        parts = [blocks[b, :, first : first + wide].astype(F32) for b in range(4)]
        total = sum(jnp.sum(p, axis=1, keepdims=True) for p in parts)
        square = sum(jnp.sum(p * p, axis=1, keepdims=True) for p in parts)
        center = total / WIDTHS[i]
        scale = lax.rsqrt(square / WIDTHS[i] - center * center + 1e-06)
        scales[:, 128 * i : 128 * i + 128] = jnp.broadcast_to(scale, (ROWS, 128))
        out = jnp.zeros((ROWS, 1024), F32)
        for b in range(4):
            value = (parts[b] - center) * scale
            xhat[b, :, first : first + wide] = value
            normed = value * gain[:, b * wide : b * wide + wide]
            out = out + dot(normed.astype(BF16), head[b * wide : b * wide + wide, :])
            lines[b, first_line : first_line + wide, :] = jnp.transpose(normed).astype(BF16)
        outs[i] = out
    for step, out in enumerate((n0, n1, n2, n3)):
        out[...] = lines[lax.rem(y + step, 4)]


def error_kernel(
    pos, hidden, sums, teacher_gain, outs, weights, xhat,
    gain_s, gain_b, gain_l, head_s, head_b, head_l,
    errors, mine, other, backs,
):
    c = pos[C]
    stats = jnp.transpose(jnp.concatenate([sums[...], jnp.zeros((120, 128), F32)], axis=0))
    center = stats[:, 0:1] / D
    spread = stats[:, 1:2] / D - center * center
    target = (hidden[...] - center) * lax.rsqrt(spread + 1e-06) * teacher_gain[...]
    target = target.astype(BF16).astype(F32)
    lane = lax.broadcasted_iota(jnp.int32, (ROWS, 64), 1)
    moments = jnp.zeros((ROWS, 64), F32)
    for i, (gain, head) in enumerate(((gain_s, head_s), (gain_b, head_b), (gain_l, head_l))):
        wide, first = QUARTERS[i], OFFSETS[i]
        weight = weights[:, 128 * i : 128 * i + 1]
        diff = outs[i] - target
        error = (weight * diff).astype(BF16)
        errors[i] = error
        loss = weight * jnp.sum(diff * diff, axis=1, keepdims=True)
        one = jnp.zeros((ROWS, 1), F32)
        two = jnp.zeros((ROWS, 1), F32)
        for b in range(4):
            back = dot_t(error, head[b * wide : b * wide + wide, :])
            value = xhat[b, :, first : first + wide]
            upper = back * gain[:, b * wide : b * wide + wide]
            one = one + jnp.sum(upper, axis=1, keepdims=True)
            two = two + jnp.sum(upper * value, axis=1, keepdims=True)
            backs[b, :, first : first + wide] = back
        moments = jnp.where(lane == 3 * i, one, jnp.where(lane == 3 * i + 1, two, moments))
        moments = jnp.where(lane == 3 * i + 2, loss, moments)
    high, low = split_sum(moments)
    turned = jnp.concatenate([high.astype(F32)[:, :32], low.astype(F32)[:, :32]], axis=1)
    zeros = jnp.zeros((ROWS, 32), F32)
    for half in range(2):
        mine[half] = backs[2 * half + c]
        mine[half, :, SPARE : SPARE + 64] = moments
        mine[half, :, BLOCK - 32 : BLOCK] = zeros
        other[half] = backs[2 * half + 1 - c].astype(BF16)
        other[half, :, SPARE : SPARE + 64] = turned.astype(BF16)
        other[half, :, BLOCK - 32 : BLOCK] = zeros.astype(BF16)


def grads_kernel(
    pos, n0, n1, n2, n3, e0, e1, e2, e3, keep, m1, m2, m3, total
):
    x = pos[X]
    for i in range(3):
        wide, first = QUARTERS[i], LINES[i]
        lines = jnp.concatenate([n[first : first + wide, :] for n in (n0, n1, n2, n3)], axis=1)
        errors = jnp.concatenate([e[i] for e in (e0, e1, e2, e3)], axis=0)
        total[first : first + wide, :] = dot(lines, errors)

    def piece(index):
        return (
            total[pl.ds(pl.multiple_of(index * 64, 8), 64), :],
            total[pl.ds(pl.multiple_of(256 + index * 48, 8), 48), :],
            total[pl.ds(pl.multiple_of(448 + index * 24, 8), 24), :],
        )

    keep[0:64, :], keep[64:112, :], keep[112:136, :] = piece(x)
    for step, out in ((1, m1), (2, m2), (3, m3)):
        large, base, small = piece(lax.rem(x + step, 4))
        out[0:64, :] = large.astype(BF16)
        out[64:112, :] = base.astype(BF16)
        out[112:144, :] = jnp.concatenate([small, jnp.zeros((8, 1024), F32)], axis=0).astype(BF16)


def back_kernel(pos, mine, got, keep, send, both):
    zh = pos[ZH]
    for half in range(2):
        both[half] = mine[half] + got[half].astype(F32)
    keep[...] = both[zh]
    send[...] = both[1 - zh].astype(BF16)
    value = both[0, :, SPARE : SPARE + 64]
    moments = value[:, 0:32] + value[:, 32:64]
    high, low = split_sum(moments)
    keep[:, SPARE : SPARE + 64] = jnp.concatenate([moments, jnp.zeros((ROWS, 32), F32)], axis=1)
    send[:, SPARE : SPARE + 64] = jnp.concatenate(
        [high.astype(F32), low.astype(F32)], axis=1
    ).astype(BF16)


def pieces_kernel(pos, keep, got, xhat, pieces):
    t = 2 * pos[ZH] + pos[C]
    back = keep[...] + got[...].astype(F32)
    moments = back[:, SPARE : SPARE + 32] + back[:, SPARE + 32 : SPARE + 64]
    terms = jnp.sum(back * xhat[t], axis=0, keepdims=True)
    pieces[...] = jnp.zeros_like(pieces)
    for j in range(5):
        pieces[j : j + 1, :] = terms[:, 128 * j : 128 * j + 128]
    pieces[5:6, 0:32] = jnp.sum(moments, axis=0, keepdims=True)


def rows_kernel(
    pos, keep, got, xhat, scales, place_t, gain_s, gain_b, gain_l, piece, piece_z, slots, gains
):
    t = 2 * pos[ZH] + pos[C]
    back = keep[...] + got[...].astype(F32)
    moments = back[:, SPARE : SPARE + 32] + back[:, SPARE + 32 : SPARE + 64]
    value = xhat[t]
    for i, gain in enumerate((gain_s, gain_b, gain_l)):
        wide = QUARTERS[i]
        for b in range(4):
            gains[b : b + 1, OFFSETS[i] : OFFSETS[i] + wide] = gain[:, b * wide : b * wide + wide]
    gain_row = gains[pl.ds(t, 1), :]
    pair = piece[...] + piece_z[...]
    high, low = split_sum(pair[5:6, 0:32])
    tail = jnp.concatenate(
        [pair[4:5], high.astype(F32), low.astype(F32), jnp.zeros((1, 64), F32)], axis=1
    )
    even = jnp.concatenate([jnp.concatenate([pair[0:1], pair[1:2]], axis=1), tail], axis=0)
    odd = jnp.concatenate([pair[2:3], pair[3:4]], axis=1)
    odd = jnp.concatenate([odd, jnp.zeros((1, 256), F32)], axis=0)
    spare = jnp.where(lax.rem(pos[ZL], 2) == 0, even, odd)
    spare = jnp.concatenate([spare, jnp.zeros((6, 256), F32)], axis=0)
    at = lax.broadcasted_iota(jnp.int32, (SHARDS * SLOT, 8), 0)
    kind = lax.broadcasted_iota(jnp.int32, (SHARDS * SLOT, 8), 1)
    ride = (lax.rem(at, SLOT) == CAP + kind).astype(F32).astype(BF16)
    slot = lax.broadcasted_iota(jnp.int32, (SHARDS * SLOT, ROWS), 0)
    total = dot(ride, spare.astype(BF16))
    for i in range(3):
        first, wide = OFFSETS[i], QUARTERS[i]
        hat = value[:, first : first + wide]
        upper = back[:, first : first + wide] * gain_row[:, first : first + wide]
        one = moments[:, 3 * i : 3 * i + 1] / WIDTHS[i]
        two = moments[:, 3 * i + 1 : 3 * i + 2] / WIDTHS[i]
        rows = scales[:, 128 * i : 128 * i + 1] * (upper - one - hat * two)
        if wide < 256:
            rows = jnp.concatenate([rows, jnp.zeros((ROWS, 256 - wide), F32)], axis=1)
        select = (slot == place_t[i : i + 1, :]).astype(F32).astype(BF16)
        total = total + dot(select, rows.astype(BF16))
    slots[...] = total.astype(BF16)


def third_kernel(pos, kept, p1, p2, p3, keep, m1, m2, m3, parts):
    zl = pos[ZL]
    total = kept[...] + sum(p[...].astype(F32)[0:136] for p in (p1, p2, p3))
    for i in range(4):
        parts[i, 0:16, :] = total[16 * i : 16 * i + 16]
        parts[i, 16:28, :] = total[64 + 12 * i : 64 + 12 * i + 12]
        parts[i, 28:34, :] = total[112 + 6 * i : 112 + 6 * i + 6]
        parts[i, 34:48, :] = jnp.zeros((14, 1024), F32)
    keep[...] = parts[zl]
    for step, out in ((1, m1), (2, m2), (3, m3)):
        out[...] = parts[lax.rem(zl + step, 4)].astype(BF16)


def last_kernel(pos, keep, m1, m2, m3, small, base, large):
    total = keep[...] + sum(p[...].astype(F32) for p in (m1, m2, m3))
    total = total / ROOT
    large[...] = total[0:16]
    base[...] = total[16:28]
    small[...] = total[28:34]


def sums_kernel(pos, got, gain_s, gain_b, gain_l, losses):
    slot = lax.broadcasted_iota(jnp.int32, (8, SHARDS * SLOT), 1)
    row = lax.broadcasted_iota(jnp.int32, (8, SHARDS * SLOT), 0)
    kind = 2 * lax.rem(lax.div(slot, SLOT), 2) + lax.rem(slot, SLOT) - CAP
    select = (lax.rem(slot, SLOT) >= CAP) & (kind == row)
    total = dot(select.astype(F32).astype(BF16), got[...])
    gain_l[...] = total[0:1] / ROOT
    gain_s[...] = total[1:2, 0:96] / ROOT
    gain_b[...] = total[2:3, 0:192] / ROOT
    loss = (total[1:2, 128:160] + total[1:2, 160:192]) / (2.0 * D * TOKENS)
    lane = lax.broadcasted_iota(jnp.int32, (1, 3), 1)
    losses[...] = jnp.where(
        lane == 0, loss[:, 2:3], jnp.where(lane == 1, loss[:, 5:6], loss[:, 8:9])
    )


def per_device(
    attn_out,
    out_proj,
    residual,
    teacher_gain,
    student_feats,
    head_small,
    head_base,
    head_large,
    gain_small,
    gain_base,
    gain_large,
    row_shard,
):
    pos = jnp.stack([lax.axis_index(a).astype(jnp.int32) for a in ("y", "x", "zl", "zh", "c")])
    tensor = 2 * pos[ZH] + pos[C]
    heads = (head_small, head_base, head_large)
    gains = (gain_small[None, :], gain_base[None, :], gain_large[None, :])

    own = out_proj.T
    early = [own] + [shifted(own, "zl", s) for s in (1, 2, 3)]
    weights = jnp.concatenate(early, axis=0)
    rows = [attn_out] + [shifted(attn_out, "y", s) for s in (1, 2, 3)]
    weights = [weights] + [shifted(weights, "x", s) for s in (1, 2, 3)]

    shard_t = jnp.pad(row_shard.T, ((0, 5), (0, 0)))
    shard_ids = jnp.arange(SHARDS, dtype=jnp.int32)
    named = (row_shard.T[:, :, None] == shard_ids[None, None, :]).astype(F32)
    own_counts = jnp.sum(named, axis=1).reshape(3 * SHARDS)
    feats = lax.dynamic_slice(student_feats, (0, tensor * 256), (SHARDS * CAP, 256))
    counts_row = jnp.pad(own_counts.astype(BF16), (0, 64))
    ride = jnp.broadcast_to(counts_row[None, None, :], (SHARDS, 2, 256))
    sent = jnp.concatenate([feats.reshape(SHARDS, CAP, 256), ride], axis=1)
    got = lax.all_to_all(sent, ("y", "x", "zl"), 0, 0, tiled=True).reshape(SHARDS * SLOT, 256)
    block, place_t, token_weights = call(
        place_kernel,
        [((ROWS, BLOCK), BF16), ((8, ROWS), jnp.int32), ((ROWS, 384), F32)],
        pos, row_shard, shard_t, got,
        flops=3 * 2 * 128 * 1024 * 256, moved=1 << 20,
    )
    block_c = swapped(block, "c")
    block_z = swapped(block, "zh")

    mine, other = call(
        teacher_kernel,
        [((2, ROWS, 1024), BF16)] * 2,
        pos, *rows, *weights,
        scratch=[((512, 1024), BF16), ((1024, 1024), BF16)],
        flops=2 * 512 * 1024 * 1024, moved=5 << 20, room=13,
    )
    first, second = call(
        pair_kernel, [((ROWS, 1024), BF16)] * 2, pos, mine, swapped(other, "c"), moved=2 << 20
    )
    parts = []
    for k, value in enumerate((first, second)):
        links = []
        for py in range(4):
            for pzh in range(2):
                for pc in range(2):
                    links.append(((py * 2 + pzh) * 2 + pc, (pc + 2 * ((pzh + k) % 2)) * 4 + py))
        parts.append(lax.ppermute(value, ("y", "zh", "c"), links))


    hidden, sums = call(
        hidden_kernel, [((ROWS, 1024), F32), ((8, ROWS), F32)], pos, *parts, residual, moved=1 << 20
    )
    block_z, hidden = lax.optimization_barrier((block_z, hidden))
    block_zc = swapped(block_z, "c")
    xhat, scales, outs, *lines = call(
        student_kernel,
        [
            ((4, ROWS, BLOCK), F32),
            ((ROWS, 384), F32),
            ((3, ROWS, 1024), F32),
        ]
        + [((544, ROWS), BF16)] * 4,
        pos, block, block_c, block_z, block_zc, *gains, *heads,
        scratch=[((4, ROWS, BLOCK), BF16), ((4, 544, ROWS), BF16)],
        flops=2 * 128 * 2176 * 1024, moved=9 << 20, room=16,
    )
    sums = sums + swapped(sums, "c")
    sums = sums + swapped(sums, "zh")

    lines = [lines[0]] + [shifted(lines[s], "y", s) for s in (1, 2, 3)]
    sums, lines = lax.optimization_barrier((sums, lines))
    errors, mine, other = call(
        error_kernel,
        [((3, ROWS, 1024), BF16), ((2, ROWS, BLOCK), F32), ((2, ROWS, BLOCK), BF16)],
        pos, hidden, sums, teacher_gain[None, :], outs, token_weights, xhat,
        *gains, *heads,
        scratch=[((4, ROWS, BLOCK), F32)],
        flops=4 * 128 * 2176 * 1024, moved=15 << 20, room=20,
    )
    errors = [errors] + [shifted(errors, "y", s) for s in (1, 2, 3)]

    got = swapped(other, "c")
    keep, send = call(
        back_kernel,
        [((ROWS, BLOCK), F32), ((ROWS, BLOCK), BF16)],
        pos, mine, got,
        scratch=[((2, ROWS, BLOCK), F32)], moved=2 << 20,
    )
    got = swapped(send, "zh")
    (pieces,) = call(pieces_kernel, [((8, 128), F32)], pos, keep, got, xhat, moved=1 << 20)
    pieces_z = lax.ppermute(pieces, "zl", [(0, 1), (1, 0), (2, 3), (3, 2)])
    (slots,) = call(
        rows_kernel,
        [((SHARDS * SLOT, 256), BF16)],
        pos, keep, got, xhat, scales, place_t, *gains, pieces, pieces_z,
        scratch=[((8, BLOCK), F32)],
        flops=3 * 2 * 128 * 1024 * 256, moved=2 << 20,
    )
    got = lax.all_to_all(slots.reshape(SHARDS, SLOT, 256), ("y", "x", "zl"), 0, 0, tiled=True)
    token_gradient = got[:, :CAP].reshape(SHARDS * CAP, 256)
    gain_s, gain_b, gain_l, losses = call(
        sums_kernel,
        [((1, n), F32) for n in (96, 192, 256, 3)],
        pos, got.reshape(SHARDS * SLOT, 256), moved=1 << 19,
    )

    keep, *sent = call(
        grads_kernel,
        [((136, 1024), F32)] + [((144, 1024), BF16)] * 3,
        pos, *lines, *errors,
        scratch=[((544, 1024), F32)], flops=2 * 512 * 544 * 1024, moved=5 << 20, room=14,
    )
    keep, *sent = call(
        third_kernel,
        [((48, 1024), F32)] + [((48, 1024), BF16)] * 3,
        pos, keep, *[shifted(sent[s - 1], "x", s) for s in (1, 2, 3)],
        scratch=[((4, 48, 1024), F32)], moved=2 << 20,
    )
    sent = [shifted(sent[s - 1], "zl", s) for s in (1, 2, 3)]
    sent, token_gradient, gain_s, gain_b, gain_l, losses = lax.optimization_barrier(
        (sent, token_gradient, gain_s, gain_b, gain_l, losses)
    )
    grad_small, grad_base, grad_large = call(
        last_kernel,
        [((6, 1024), F32), ((12, 1024), F32), ((16, 1024), F32)],
        pos, keep, *sent,
        moved=1 << 20,
    )
    return (
        grad_small,
        grad_base,
        grad_large,
        gain_s[0],
        gain_b[0],
        gain_l[0],
        token_gradient,
        losses[0],
    )


def solution(mesh):
    fine = Mesh(mesh.devices.reshape(4, 4, 4, 2, 2), ("y", "x", "zl", "zh", "c"))
    dp = ("y", "x", "zl")
    tp = ("zh", "c")
    return jax.shard_map(
        per_device,
        mesh=fine,
        in_specs=(
            P(dp, tp),
            P(tp, dp),
            P(dp, tp),
            P(tp),
            P(dp, None),
            P(None, tp),
            P(None, tp),
            P(None, tp),
            P(),
            P(),
            P(),
            P(dp, None),
        ),
        out_specs=(
            P(dp, tp),
            P(dp, tp),
            P(dp, tp),
            P(tp),
            P(tp),
            P(tp),
            P(dp, tp),
            P(),
        ),
        check_vma=False,
    )
```
